256 devices in a mesh: grp: 8 (over x, core), sec: 32 (over y, z).
Axes of the slice: x: 4, y: 4, z: 8, core: 2. Of those that a mesh axis runs over, the one named last changes fastest.
Arguments:
- left_env: bfloat16 [8, 2, 16384, 512], P('grp', None, 'sec'), may hold values from -0.09375 to 0.09375
- right_env: bfloat16 [8, 2, 16384, 512], P('grp', None, 'sec'), may hold values from -0.25 to 0.25
- guess: float32 [16384, 512], P('sec'), may hold values from -6 to 6
- precond: float32 [16384, 512], P('sec'), may hold values from 0.1 to 1
- sector_rows: int32 [32], P('sec'), may hold values from 128 to 512, as said below
Outputs:
- ritz_vector: float32 [16384, 512], P('sec')
- energies: float32 [3], replicated
The draws below stay inside these ranges and needn't reach their ends.
Inputs may be any that keep to these rules, and one draw needn't show every extreme that they name: `sector_rows`: every entry is a multiple of 128; some sector uses all 512 rows.
All inputs are finite; a program needn't handle non-finite values.
Results may differ from the reference program's by a relative error of at most 0.02.
Values may be sent and summed in bfloat16 or wider, within the bound.
A program may use at most 64 MiB of HBM per device.

```python
import math
import jax
import jax.numpy as jnp
from jax import lax

B = 512
ROW_UNIT = 128
CHARGES = 2
ITERS = 3
GROUPS = 8
SECTORS = 32
BOND = 16384
N_GRP = 8


def draw_sector_rows(key, part):
    key = jax.random.fold_in(key, 7)
    first_key, second_key = jax.random.split(key)
    units = jax.random.randint(first_key, (SECTORS,), 1, B // ROW_UNIT + 1)
    spot = jax.random.randint(second_key, (), 0, SECTORS)
    units = jnp.where(jnp.arange(SECTORS) == spot, B // ROW_UNIT, units)
    return (units * ROW_UNIT).astype(jnp.int32)


def steps_of(stream_key, extent, shards, least, high):
    def one(position, shards_of):
        heights = jax.random.uniform(jax.random.fold_in(jax.random.fold_in(stream_key, 6), position), (shards_of,), jnp.float32, least / len(shards), high / len(shards))
        return jnp.repeat(jnp.exp(heights), extent[position] // shards_of).reshape((-1,) + (1,) * (len(extent) - position - 1))

    gain = one(*shards[0])
    for cut in shards[1:]:
        gain = gain * one(*cut)
    return gain


def noise(stream_key, extent, deviation, bound, pieces=(), dtype=jnp.bfloat16):
    entries = jax.random.normal(stream_key, extent, jnp.float32) * deviation
    if len(pieces) > 0:
        entries = steps_of(stream_key, extent, pieces, -0.22, 0.18) * entries
    return jnp.clip(entries, min=-bound, max=bound).astype(dtype)


def setup_inputs(seed: int = 0) -> dict:
    keys = jax.random.split(jax.random.key(seed), 6)
    return {
        "left_env": noise(keys[0], (GROUPS, CHARGES, BOND, B), (B * N_GRP) ** -0.5, 0.09375, ((0, 8), (2, 32))),
        "right_env": noise(keys[1], (GROUPS, CHARGES, BOND, B), B ** -0.5, 0.25, ((0, 8), (2, 32))),
        "guess": noise(keys[2], (BOND, B), 1.0, 6.0, ((0, 32),), jnp.float32),
        "precond": jnp.clip(jnp.exp(math.log(1.0) - 2.3025851 * jax.random.uniform(keys[3], (BOND, B), jnp.float32) ** steps_of(keys[3], (BOND, B), ((0, 32),), -0.2, 0.2)), 0.1, 1.0),
        "sector_rows": draw_sector_rows(jax.random.fold_in(keys[5], 71), 0),
    }


def round_keep(values):
    return lax.optimization_barrier(values.astype(jnp.bfloat16)).astype(jnp.float32)

def reference(left_env, right_env, guess, precond, sector_rows):
    row_ids = lax.iota(jnp.int32, B)
    inside = row_ids[None, :] < sector_rows[:, None]
    mask = (inside[:, :, None] & inside[:, None, :]).astype(jnp.float32)

    def operate(vector):
        rounded = round_keep(vector)
        result = jnp.zeros((SECTORS, B, B), jnp.float32)
        for group in range(GROUPS):
            for charge in range(CHARGES):
                left = left_env[group, charge].reshape(SECTORS, B, B).astype(jnp.float32)
                right = right_env[group, charge].reshape(SECTORS, B, B).astype(jnp.float32)
                inner = round_keep(jnp.einsum('sij,sjk->sik', rounded, right))
                raised = jnp.einsum('sij,sjk->sik', left, inner)
                if charge > 0:
                    blank = jnp.zeros((charge, B, B), jnp.float32)
                    raised = jnp.concatenate([blank, raised[:SECTORS - charge]], axis=0)
                    source = jnp.concatenate([rounded[charge:], blank], axis=0)
                else:
                    source = rounded
                inner_two = round_keep(jnp.einsum('sij,skj->sik', source, right))
                lowered = jnp.einsum('sji,sjk->sik', left, inner_two)
                result = result + raised + lowered
        return result * mask
    start = mask * guess.reshape(SECTORS, B, B)
    weights = precond.reshape(SECTORS, B, B)
    vector = start / jnp.sqrt(jnp.sum(start * start))
    image = operate(vector)
    ritz = jnp.sum(vector * image)
    found = []
    for step in range(ITERS):
        resid = image - ritz * vector
        corr = weights * resid
        along = jnp.sum(vector * corr)
        ortho = corr - along * vector
        normed = ortho / jnp.sqrt(jnp.sum(ortho * ortho))
        image_two = operate(normed)
        couple = jnp.sum(normed * image)
        diag_two = jnp.sum(normed * image_two)
        theta = (ritz + diag_two) / 2.0 - jnp.sqrt(((ritz - diag_two) / 2.0) ** 2 + couple ** 2)
        length = jnp.sqrt((diag_two - theta) ** 2 + couple ** 2)
        first_coef = (diag_two - theta) / length
        second_coef = -couple / length
        vector = first_coef * vector + second_coef * normed
        image = first_coef * image + second_coef * image_two
        ritz = theta
        found.append(theta)
    scaled = vector * math.sqrt(float(BOND * B))
    return (scaled.reshape(BOND, B), jnp.stack(found))
```

```python
import functools
import math

import jax
import jax.numpy as jnp
from jax import lax
from jax.experimental import pallas as pl
from jax.experimental.pallas import tpu as pltpu
from jax.sharding import PartitionSpec as P

ITERS = 3
B = 512
HALF = 256
Q = 128
NX = 4
NY = 4
MESH = pl.DeviceIdType.MESH
F32 = jnp.float32
BF16 = jnp.bfloat16


def rows_of(j):
    return pl.ds(pl.multiple_of(j * Q, Q), Q)


def dot(a, b):
    return jnp.dot(a, b, preferred_element_type=F32)


def fold(values):
    total = values[:, 0:128]
    for k in range(1, values.shape[1] // 128):
        total = total + values[:, k * 128 : (k + 1) * 128]
    return jnp.sum(total, axis=0, keepdims=True)


def kernel(
    sectors, ny, nz,
    left, right, guess, precond, used_ref,
    out, energies,
    lr, lo, rt, ru, rraw,
    kw, kw16, kup, xsend,
    x, h, t, xu, hu, tu, tb, tub,
    gown, gup, so, sr, ro, rr,
    acc, praise, in1, inn, keep_own,
    sc_c, sc_x, sc_y, sc_z, coef,
    load_sem, env_s, env_r, k_s, k_r,
    up_s, up_r, upc_s, upc_r, own_s, own_r, ownc_s, ownc_r,
    so_s, ro_r, sr_s, rr_r,
    scc_s, scc_r, scx_s, scx_r, scy_s, scy_r, scz_s, scz_r,
):
    g = lax.axis_index("grp")
    s = lax.axis_index("sec")
    px, c = g // 2, g % 2
    py, pz = s // nz, s % nz
    above = lax.rem(s + 1, sectors)
    below = lax.rem(s + sectors - 1, sectors)
    other = 1 - c
    partner = (px * 2 + other, s)
    mine = pl.ds(pl.multiple_of(c * HALF, HALF), HALF)
    theirs = pl.ds(pl.multiple_of(other * HALF, HALF), HALF)

    def xdev(j, sec):
        return (j * 2 + c, sec)

    def xoff(k):
        return lax.rem(px + k, NX)

    def rcopy(src, dst, ssem, rsem, dev):
        return pltpu.make_async_remote_copy(
            src_ref=src, dst_ref=dst, send_sem=ssem, recv_sem=rsem, device_id=dev, device_id_type=MESH
        )

    loads = [
        (right.at[0, 1, :, mine], rt.at[:, 0:256]),
        (left.at[0, 1], lr.at[:, 0:512]),
        (right.at[0, 0, :, mine], rt.at[:, 512:768]),
        (left.at[0, 0], lo.at[:, 0:512]),
        (right.at[0, 0, mine, :], rraw.at[0]),
        (right.at[0, 1, mine, :], rraw.at[2]),
        (guess.at[:, 0:256], t.at[0]),
        (guess.at[:, 256:512], t.at[1]),
        (precond.at[:, 0:256], kw.at[0]),
        (precond.at[:, 256:512], kw.at[1]),
    ]
    local = [pltpu.make_async_copy(a, b, load_sem.at[i]) for i, (a, b) in enumerate(loads)]
    for i in (6, 7, 1, 0, 3, 2, 4, 5, 8, 9):
        local[i].start()

    barrier = pltpu.get_barrier_semaphore()
    peers = [partner]
    peers += [xdev(xoff(k), s) for k in range(1, NX)]
    peers += [xdev(xoff(k), above) for k in range(NX)]
    peers += [xdev(xoff(k), below) for k in range(NX)]
    peers += [(g, lax.rem(py + k, ny) * nz + pz) for k in range(1, ny)]
    peers += [(g, py * nz + lax.rem(pz + k, nz)) for k in range(1, nz)]
    for peer in peers:
        pl.semaphore_signal(barrier, inc=1, device_id=peer, device_id_type=MESH)

    used = used_ref[0]
    row_ids = lax.broadcasted_iota(jnp.int32, (Q, HALF), 0)
    col_ids = lax.broadcasted_iota(jnp.int32, (Q, HALF), 1)

    def mask_of(j, half):
        return ((row_ids + j * Q < used) & (col_ids + half * HALF < used)).astype(F32)

    local[6].wait()
    local[7].wait()

    def start_rows(j, _):
        for half in range(2):
            value = t[half, rows_of(j)] * mask_of(j, half)
            t[half, rows_of(j)] = value
            x[half, rows_of(j)] = jnp.zeros((Q, HALF), F32)
            h[half, rows_of(j)] = jnp.zeros((Q, HALF), F32)
            rounded = value.astype(BF16)
            tb[rows_of(j), half * HALF : (half + 1) * HALF] = rounded
            xsend[half, rows_of(j)] = rounded
        return 0

    lax.fori_loop(0, NX, start_rows, 0)
    pl.semaphore_wait(barrier, len(peers))

    def up_start(j, _):
        rcopy(
            xsend.at[c, rows_of(j)], gup.at[0, c, rows_of(j)], up_s.at[0, j], up_r.at[0, j], (g, below)
        ).start()
        return 0

    lax.fori_loop(0, NX, up_start, 0)
    envs = [
        (left.at[0, 1], lr.at[:, 512:1024]),
        (right.at[0, 1, :, theirs], rt.at[:, 256:512]),
        (left.at[0, 0], lo.at[:, 512:1024]),
        (right.at[0, 0, :, theirs], rt.at[:, 768:1024]),
        (right.at[0, 0, theirs, :], rraw.at[1]),
        (right.at[0, 1, theirs, :], rraw.at[3]),
    ]
    env = [rcopy(a, b, env_s.at[i], env_r.at[i], partner) for i, (a, b) in enumerate(envs)]
    for copy in env:
        copy.start()

    for i in (0, 1, 2, 3, 4, 5, 8, 9):
        local[i].wait()

    def k_rows(j, _):
        for half in range(2):
            kw16[half, rows_of(j)] = kw[half, rows_of(j)].astype(BF16)
        return 0

    lax.fori_loop(0, NX, k_rows, 0)
    k_copy = rcopy(kw16, kup, k_s, k_r, (g, below))

    has_above = (s < sectors - 1).astype(F32)

    def gate(values):
        return (values.astype(F32) * has_above).astype(BF16)

    lo[:, 1024:1536] = lo[:, 0:512].T
    lo[:, 2048:2560] = lr[:, 0:512].T
    rt[:, 0:256] = gate(rt[:, 0:256])
    rt[:, 1024:1280] = rraw[0].T
    ru[:, 0:256] = gate(rraw[2].T)
    for copy in env:
        copy.wait_recv()
    lo[:, 1536:2048] = lo[:, 512:1024].T
    lo[:, 2560:3072] = lr[:, 512:1024].T
    rt[:, 256:512] = gate(rt[:, 256:512])
    rt[:, 1280:1536] = rraw[1].T
    ru[:, 256:512] = gate(rraw[3].T)

    def upper_forward(r):
        def one(j, _):
            rcopy(
                gup.at[r, c, rows_of(j)], gup.at[r, c, rows_of(j)], up_s.at[r, j], up_r.at[r, j], partner
            ).wait_recv()
            rcopy(
                gup.at[r, c, rows_of(j)], gup.at[r, c, rows_of(j)], upc_s.at[r, j], upc_r.at[r, j], partner
            ).start()
            return 0

        lax.fori_loop(0, NX, one, 0)

    def upper_update(r):
        def wait(j):
            rcopy(
                gup.at[r, c, rows_of(j)], gup.at[r, other, rows_of(j)], upc_s.at[r, j], upc_r.at[r, j], partner
            ).wait_recv()

        @pl.when(r == 0)
        def _():
            def one(j, _):
                wait(j)
                for half in range(2):
                    got = gup[0, half, rows_of(j)]
                    tub[rows_of(j), half * HALF : (half + 1) * HALF] = got
                    tu[half, rows_of(j)] = got.astype(F32)
                    xu[half, rows_of(j)] = jnp.zeros((Q, HALF), F32)
                    hu[half, rows_of(j)] = jnp.zeros((Q, HALF), F32)
                return 0

            lax.fori_loop(0, NX, one, 0)
            k_copy.start()

        @pl.when(r == 1)
        def _():
            k_copy.wait_recv()

        @pl.when(r > 0)
        def _():
            a0, d0, ritz = coef[0], coef[1], coef[2]

            def one(j, _):
                wait(j)
                for half in range(2):
                    new_x = a0 * xu[half, rows_of(j)] + d0 * tu[half, rows_of(j)]
                    new_h = a0 * hu[half, rows_of(j)] + d0 * gup[r, half, rows_of(j)].astype(F32)
                    new_t = kup[half, rows_of(j)].astype(F32) * (new_h - ritz * new_x)
                    xu[half, rows_of(j)] = new_x
                    hu[half, rows_of(j)] = new_h
                    tu[half, rows_of(j)] = new_t
                    tub[rows_of(j), half * HALF : (half + 1) * HALF] = new_t.astype(BF16)
                return 0

            lax.fori_loop(0, NX, one, 0)

    def local_sums(extra):
        xb, tv, hb = x[c, rows_of(px)], t[c, rows_of(px)], h[c, rows_of(px)]
        return jnp.concatenate(
            [
                fold(xb * tv), fold(tv * tv), fold(tv * hb), extra,
                fold(xb * xb), fold(xb * hb), jnp.zeros((2, 128), F32),
            ],
            axis=0,
        )

    def stage(buf, ssem, rsem, size, me, dev_of):
        def send(r, value):
            buf[r, me] = value
            for k in range(1, size):
                rcopy(
                    buf.at[r, me], buf.at[r, me], ssem.at[r, k], rsem.at[r, me], dev_of(lax.rem(me + k, size))
                ).start()

        def finish(r):
            for k in range(1, size):
                src = lax.rem(me + k, size)
                rcopy(buf.at[r, me], buf.at[r, src], ssem.at[r, k], rsem.at[r, src], dev_of(src)).wait_recv()
            total = buf[r, 0]
            for k in range(1, size):
                total = total + buf[r, k]
            return total

        def drain(r):
            for k in range(1, size):
                rcopy(
                    buf.at[r, me], buf.at[r, me], ssem.at[r, k], rsem.at[r, me], dev_of(lax.rem(me + k, size))
                ).wait_send()

        return send, finish, drain

    c_send, c_finish, c_drain = stage(sc_c, scc_s, scc_r, 2, c, lambda i: (px * 2 + i, s))
    x_send, x_finish, x_drain = stage(sc_x, scx_s, scx_r, NX, px, lambda i: (i * 2 + c, s))
    y_send, y_finish, y_drain = stage(sc_y, scy_s, scy_r, ny, py, lambda i: (g, i * nz + pz))
    z_send, z_finish, z_drain = stage(sc_z, scz_s, scz_r, nz, pz, lambda i: (g, py * nz + i))

    def coefficients(total, r, ritz):
        sums = jnp.sum(total, axis=1, keepdims=True)
        xt, tt, th, tat, xx, xh = (sums[k : k + 1, 0:1] for k in range(6))
        norm = jnp.sqrt(tt)
        start = (jnp.zeros_like(norm), 1.0 / norm, tat / tt)
        n2 = tt - 2.0 * xt * xt + xt * xt * xx
        n = jnp.sqrt(n2)
        couple = (th - xt * xh) / n
        diag = (tat - 2.0 * xt * th + xt * xt * xh) / n2
        theta = (ritz + diag) / 2.0 - jnp.sqrt(((ritz - diag) / 2.0) ** 2 + couple**2)
        length = jnp.sqrt((diag - theta) ** 2 + couple**2)
        first = (diag - theta) / length
        second = -couple / length
        later = (first - second * xt / n, second / n, theta)
        return [jnp.where(r == 0, u, v) for u, v in zip(start, later)]

    def set_coef(total, r, ritz):
        a0, d0, new = coefficients(total, r, ritz)
        coef[0] = a0[0, 0]
        coef[1] = d0[0, 0]
        coef[2] = new[0, 0]
        return new

    def raise_inner():
        inner = dot(tb[...], rt[:, 0:512])
        in1[0:512] = inner[:, 0:256].astype(BF16)
        in1[512:1024] = inner[:, 256:512].astype(BF16)

    def round_body(r, ritz):
        raise_inner()

        def raise_rows(k, _):
            j = xoff(k + 2)
            value = dot(lr[rows_of(j)], in1[...])
            praise[rows_of(j)] = value
            sr[r, rows_of(j)] = value.astype(BF16)
            rcopy(sr.at[r, rows_of(j)], rr.at[r, px], sr_s.at[r, j], rr_r.at[r, px], xdev(j, above)).start()
            return 0

        lax.fori_loop(0, NX, raise_rows, 0)
        upper_forward(r)

        for k in range(4):
            inn[k * 512 : (k + 1) * 512] = dot(tb[...], rt[:, 512 + k * 256 : 768 + k * 256]).astype(BF16)

        def own_rows(j, part):
            value = dot(lo[rows_of(j), 0:2048], inn[0:2048])
            acc[rows_of(j)] = value
            return part + fold(value * t[c, rows_of(j)])

        part = lax.fori_loop(0, NX, own_rows, jnp.zeros((1, 128), F32))

        upper_update(r)
        for k in range(2):
            inn[2048 + k * 512 : 2560 + k * 512] = dot(tub[...], ru[:, k * 256 : (k + 1) * 256]).astype(BF16)

        def raise_part(j, total):
            return total + 2.0 * fold(praise[rows_of(j)] * tu[c, rows_of(j)])

        part = lax.fori_loop(0, NX, raise_part, part)
        c_send(r, local_sums(part))

        def lower_rows(k, _):
            j = xoff(k + 2)
            value = acc[rows_of(j)] + dot(lo[rows_of(j), 2048:3072], inn[2048:3072])

            @pl.when(j == px)
            def _():
                keep_own[...] = value

            @pl.when(j != px)
            def _():
                so[r, rows_of(j)] = value.astype(BF16)
                rcopy(so.at[r, rows_of(j)], ro.at[r, px], so_s.at[r, j], ro_r.at[r, px], xdev(j, s)).start()

            return 0

        lax.fori_loop(0, NX, lower_rows, 0)
        x_send(r, c_finish(r))

        def raised_in(j, _):
            rcopy(sr.at[r, rows_of(j)], rr.at[r, j], sr_s.at[r, j], rr_r.at[r, j], xdev(j, below)).wait_recv()
            return 0

        def own_in(k, _):
            j = xoff(k)
            rcopy(so.at[r, rows_of(j)], ro.at[r, j], so_s.at[r, j], ro_r.at[r, j], xdev(j, s)).wait_recv()
            return 0

        y_send(r, x_finish(r))
        lax.fori_loop(1, NX, own_in, 0)
        value = keep_own[...]
        for k in range(1, NX):
            value = value + ro[r, xoff(k)].astype(F32)
        lax.fori_loop(0, NX, raised_in, 0)
        for k in range(NX):
            value = value + rr[r, k].astype(F32)
        block = (value * mask_of(px, c)).astype(BF16)
        gown[r, c, rows_of(px)] = block

        home = gown.at[r, c, rows_of(px)]
        rcopy(home, home, ownc_s.at[r, px], ownc_r.at[r, px], partner).start()
        for k in (2, 1, 3):
            j = xoff(k)
            rcopy(home, home, own_s.at[r, k], own_r.at[r, px], xdev(j, s)).start()
        for k in (2, 1, 3, 0):
            j = xoff(k)
            rcopy(
                home, gup.at[r + 1, c, rows_of(px)], up_s.at[r + 1, k], up_r.at[r + 1, px], xdev(j, below)
            ).start()

        z_send(r, y_finish(r))

        for k in (1, 3, 2):
            there = gown.at[r, c, rows_of(xoff(k))]
            rcopy(there, there, own_s.at[r, k], own_r.at[r, xoff(k)], partner).wait_recv()
            rcopy(there, there, ownc_s.at[r, xoff(k)], ownc_r.at[r, xoff(k)], partner).start()

        new_ritz = set_coef(z_finish(r), r, ritz)

        @pl.when(r > 0)
        def _():
            energies[r - 1] = coef[2]

        a0, d0, theta = coef[0], coef[1], coef[2]

        def update(k, _):
            j = xoff(k)
            there = gown.at[r, other, rows_of(j)]
            rcopy(there, there, ownc_s.at[r, j], ownc_r.at[r, j], partner).wait_recv()
            for half in range(2):
                new_x = a0 * x[half, rows_of(j)] + d0 * t[half, rows_of(j)]
                new_h = a0 * h[half, rows_of(j)] + d0 * gown[r, half, rows_of(j)].astype(F32)
                new_t = kw[half, rows_of(j)] * (new_h - theta * new_x)
                x[half, rows_of(j)] = new_x
                h[half, rows_of(j)] = new_h
                t[half, rows_of(j)] = new_t
                tb[rows_of(j), half * HALF : (half + 1) * HALF] = new_t.astype(BF16)
            return 0

        lax.fori_loop(0, NX, update, 0)
        return new_ritz

    ritz = lax.fori_loop(0, ITERS, round_body, jnp.zeros((1, 1), F32))

    last = ITERS
    raise_inner()
    inn[0:512] = dot(tb[...], rt[:, 512:768]).astype(BF16)
    inn[512:1024] = dot(tb[...], rt[:, 768:1024]).astype(BF16)

    def last_rows(j, part):
        praise[rows_of(j)] = dot(lr[rows_of(j)], in1[...])
        return part + 2.0 * fold(dot(lo[rows_of(j), 0:1024], inn[0:1024]) * t[c, rows_of(j)])

    part = lax.fori_loop(0, NX, last_rows, jnp.zeros((1, 128), F32))
    upper_forward(last)
    upper_update(last)

    def last_part(j, total):
        return total + 2.0 * fold(praise[rows_of(j)] * tu[c, rows_of(j)])

    part = lax.fori_loop(0, NX, last_part, part)
    c_send(last, local_sums(part))
    x_send(last, c_finish(last))

    def drain_round(r, _):
        def rows(j, _):
            rcopy(sr.at[r, rows_of(j)], rr.at[r, px], sr_s.at[r, j], rr_r.at[r, px], xdev(j, above)).wait_send()
            home = gown.at[r, c, rows_of(px)]
            rcopy(home, home, ownc_s.at[r, j], ownc_r.at[r, px], partner).wait_send()
            return 0

        def others(k, _):
            j = xoff(k)
            rcopy(so.at[r, rows_of(j)], ro.at[r, px], so_s.at[r, j], ro_r.at[r, px], xdev(j, s)).wait_send()
            home = gown.at[r, c, rows_of(px)]
            rcopy(home, home, own_s.at[r, k], own_r.at[r, px], xdev(j, s)).wait_send()
            return 0

        lax.fori_loop(0, NX, rows, 0)
        lax.fori_loop(1, NX, others, 0)
        return 0

    def drain_upper(r, _):
        def rows(j, _):
            there = gup.at[r, c, rows_of(j)]
            rcopy(there, there, up_s.at[r, j], up_r.at[r, j], (g, below)).wait_send()
            rcopy(there, there, upc_s.at[r, j], upc_r.at[r, j], partner).wait_send()
            return 0

        lax.fori_loop(0, NX, rows, 0)
        return 0

    lax.fori_loop(0, ITERS, drain_round, 0)
    lax.fori_loop(0, ITERS + 1, drain_upper, 0)
    for copy in env:
        copy.wait_send()
    k_copy.wait_send()

    y_send(last, x_finish(last))
    z_send(last, y_finish(last))
    set_coef(z_finish(last), last, ritz)
    energies[last - 1] = coef[2]
    scale = math.sqrt(float(B * B * sectors))
    a0, d0 = coef[0] * scale, coef[1] * scale

    def write(j, _):
        for half in range(2):
            out[rows_of(j), half * HALF : (half + 1) * HALF] = a0 * x[half, rows_of(j)] + d0 * t[half, rows_of(j)]
        return 0

    lax.fori_loop(0, NX, write, 0)

    def drain_sums(r, _):
        for drain in (c_drain, x_drain, y_drain, z_drain):
            drain(r)
        return 0

    lax.fori_loop(0, ITERS + 1, drain_sums, 0)


def body(left_env, right_env, guess, precond, sector_rows):
    sectors = lax.axis_size("sec")
    ny = min(NY, sectors)
    nz = sectors // ny
    rounds = ITERS + 1
    vm, dma = pltpu.VMEM, pltpu.SemaphoreType.DMA
    halves = (2, B, HALF)
    scratch = [
        vm((B, 1024), BF16), vm((B, 3072), BF16), vm((B, 1536), BF16), vm((B, 512), BF16), vm((4, HALF, B), BF16),
        vm(halves, F32), vm(halves, BF16), vm(halves, BF16), vm(halves, BF16),
        vm(halves, F32), vm(halves, F32), vm(halves, F32), vm(halves, F32), vm(halves, F32), vm(halves, F32),
        vm((B, B), BF16), vm((B, B), BF16),
        vm((ITERS,) + halves, BF16), vm((rounds,) + halves, BF16),
        vm((ITERS, B, HALF), BF16), vm((ITERS, B, HALF), BF16),
        vm((ITERS, NX, Q, HALF), BF16), vm((ITERS, NX, Q, HALF), BF16),
        vm((B, HALF), F32), vm((B, HALF), F32), vm((1024, HALF), BF16), vm((3072, HALF), BF16), vm((Q, HALF), F32),
        vm((rounds, 2, 8, 128), F32), vm((rounds, NX, 8, 128), F32),
        vm((rounds, ny, 8, 128), F32), vm((rounds, nz, 8, 128), F32),
        pltpu.SMEM((4,), F32),
        dma((10,)), dma((6,)), dma((6,)), dma, dma,
        dma((rounds, NX)), dma((rounds, NX)), dma((rounds, NX)), dma((rounds, NX)),
        dma((ITERS, NX)), dma((ITERS, NX)), dma((ITERS, NX)), dma((ITERS, NX)),
        dma((ITERS, NX)), dma((ITERS, NX)), dma((ITERS, NX)), dma((ITERS, NX)),
        dma((rounds, 2)), dma((rounds, 2)), dma((rounds, NX)), dma((rounds, NX)),
        dma((rounds, ny)), dma((rounds, ny)), dma((rounds, nz)), dma((rounds, nz)),
    ]
    any_space = pl.BlockSpec(memory_space=pl.ANY)
    return pl.pallas_call(
        functools.partial(kernel, sectors, ny, nz),
        out_shape=(jax.ShapeDtypeStruct((B, B), F32), jax.ShapeDtypeStruct((ITERS,), F32)),
        in_specs=[any_space] * 4 + [pl.BlockSpec(memory_space=pltpu.SMEM)],
        out_specs=(pl.BlockSpec(memory_space=pltpu.VMEM), pl.BlockSpec(memory_space=pltpu.SMEM)),
        scratch_shapes=scratch,
        compiler_params=pltpu.CompilerParams(
            collective_id=0, has_side_effects=True, vmem_limit_bytes=56 * 1024 * 1024
        ),
        name="davidson",
    )(left_env, right_env, guess, precond, sector_rows)


def solution(mesh):
    in_specs = (
        P("grp", None, "sec", None),
        P("grp", None, "sec", None),
        P("sec", None),
        P("sec", None),
        P("sec"),
    )
    out_specs = (P("sec", None), P())
    return jax.shard_map(body, mesh=mesh, in_specs=in_specs, out_specs=out_specs, check_vma=False)
```

```python
import functools
import math

import jax
import jax.numpy as jnp
from jax import lax
from jax.experimental import pallas as pl
from jax.experimental.pallas import tpu as pltpu
from jax.sharding import PartitionSpec as P

ITERS = 3
B = 512
HALF = 256
Q = 128
NX = 4
NY = 4
MESH = pl.DeviceIdType.MESH
F32 = jnp.float32
BF16 = jnp.bfloat16


def rows_of(j):
    return pl.ds(pl.multiple_of(j * Q, Q), Q)


def dot(a, b):
    return jnp.dot(a, b, preferred_element_type=F32)


def fold(values):
    total = values[:, 0:128]
    for k in range(1, values.shape[1] // 128):
        total = total + values[:, k * 128 : (k + 1) * 128]
    return jnp.sum(total, axis=0, keepdims=True)


def kernel(
    sectors, ny, nz,
    left, right, guess, precond, used_ref,
    out, energies,
    lr, lo, rt, ru, rraw,
    kw, kw16, kup, xsend,
    x, h, t, xu, hu, tu, tb, tub,
    gown, gup, so, sr, ro, rr,
    acc, praise, in1, inn, keep_own,
    sc_c, sc_x, sc_y, sc_z, coef,
    load_sem, env_s, env_r, k_s, k_r,
    up_s, up_r, upc_s, upc_r, own_s, own_r, ownc_s, ownc_r,
    so_s, ro_r, sr_s, rr_r,
    scc_s, scc_r, scx_s, scx_r, scy_s, scy_r, scz_s, scz_r,
):
    g = lax.axis_index("grp")
    s = lax.axis_index("sec")
    px, c = g // 2, g % 2
    py, pz = s // nz, s % nz
    above = lax.rem(s + 1, sectors)
    below = lax.rem(s + sectors - 1, sectors)
    other = 1 - c
    partner = (px * 2 + other, s)
    mine = pl.ds(pl.multiple_of(c * HALF, HALF), HALF)
    theirs = pl.ds(pl.multiple_of(other * HALF, HALF), HALF)

    def xdev(j, sec):
        return (j * 2 + c, sec)

    def xoff(k):
        return lax.rem(px + k, NX)

    def rcopy(src, dst, ssem, rsem, dev):
        return pltpu.make_async_remote_copy(
            src_ref=src, dst_ref=dst, send_sem=ssem, recv_sem=rsem, device_id=dev, device_id_type=MESH
        )

    loads = [
        (right.at[0, 1, :, mine], rt.at[:, 0:256]),
        (left.at[0, 1], lr.at[:, 0:512]),
        (right.at[0, 0, :, mine], rt.at[:, 512:768]),
        (left.at[0, 0], lo.at[:, 0:512]),
        (right.at[0, 0, mine, :], rraw.at[0]),
        (right.at[0, 1, mine, :], rraw.at[2]),
        (guess.at[:, 0:256], t.at[0]),
        (guess.at[:, 256:512], t.at[1]),
        (precond.at[:, 0:256], kw.at[0]),
        (precond.at[:, 256:512], kw.at[1]),
    ]
    local = [pltpu.make_async_copy(a, b, load_sem.at[i]) for i, (a, b) in enumerate(loads)]
    for i in (6, 7, 1, 0, 3, 2, 4, 5, 8, 9):
        local[i].start()

    barrier = pltpu.get_barrier_semaphore()
    peers = [partner]
    peers += [xdev(xoff(k), s) for k in range(1, NX)]
    peers += [(g, above), (g, below)]
    peers += [(g, lax.rem(py + k, ny) * nz + pz) for k in range(1, ny)]
    peers += [(g, py * nz + lax.rem(pz + k, nz)) for k in range(1, nz)]
    for peer in peers:
        pl.semaphore_signal(barrier, inc=1, device_id=peer, device_id_type=MESH)

    used = used_ref[0]
    row_ids = lax.broadcasted_iota(jnp.int32, (Q, HALF), 0)
    col_ids = lax.broadcasted_iota(jnp.int32, (Q, HALF), 1)

    def mask_of(j, half):
        return ((row_ids + j * Q < used) & (col_ids + half * HALF < used)).astype(F32)

    local[6].wait()
    local[7].wait()

    def start_rows(j, _):
        for half in range(2):
            value = t[half, rows_of(j)] * mask_of(j, half)
            t[half, rows_of(j)] = value
            x[half, rows_of(j)] = jnp.zeros((Q, HALF), F32)
            h[half, rows_of(j)] = jnp.zeros((Q, HALF), F32)
            rounded = value.astype(BF16)
            tb[rows_of(j), half * HALF : (half + 1) * HALF] = rounded
            xsend[half, rows_of(j)] = rounded
        return 0

    lax.fori_loop(0, NX, start_rows, 0)
    pl.semaphore_wait(barrier, len(peers))

    def up_start(j, _):
        rcopy(
            xsend.at[c, rows_of(j)], gup.at[0, c, rows_of(j)], up_s.at[0, j], up_r.at[0, j], (g, below)
        ).start()
        return 0

    lax.fori_loop(0, NX, up_start, 0)
    envs = [
        (left.at[0, 1], lr.at[:, 512:1024]),
        (right.at[0, 1, :, theirs], rt.at[:, 256:512]),
        (left.at[0, 0], lo.at[:, 512:1024]),
        (right.at[0, 0, :, theirs], rt.at[:, 768:1024]),
        (right.at[0, 0, theirs, :], rraw.at[1]),
        (right.at[0, 1, theirs, :], rraw.at[3]),
    ]
    env = [rcopy(a, b, env_s.at[i], env_r.at[i], partner) for i, (a, b) in enumerate(envs)]
    for copy in env:
        copy.start()

    k_copy = rcopy(kw16.at[c], kup.at[c], k_s.at[0], k_r.at[0], (g, below))
    k_forward = rcopy(kup.at[c], kup.at[c], k_s.at[1], k_r.at[1], partner)

    has_above = (s < sectors - 1).astype(F32)

    def gate(values):
        return (values.astype(F32) * has_above).astype(BF16)

    def ready_raise():
        local[0].wait()
        local[1].wait()
        env[0].wait_recv()
        env[1].wait_recv()
        rt[:, 0:512] = gate(rt[:, 0:512])

    def ready_own():
        for i in (2, 3, 4):
            local[i].wait()
        rt[:, 1024:1280] = rraw[0].T
        lo[:, 1024:1536] = lo[:, 0:512].T
        for i in (2, 3, 4):
            env[i].wait_recv()
        rt[:, 1280:1536] = rraw[1].T
        lo[:, 1536:2048] = lo[:, 512:1024].T

    def ready_lower():
        local[5].wait()
        ru[:, 0:256] = gate(rraw[2].T)
        lo[:, 2048:2560] = lr[:, 0:512].T
        env[5].wait_recv()
        ru[:, 256:512] = gate(rraw[3].T)
        lo[:, 2560:3072] = lr[:, 512:1024].T

    def ready_weights():
        local[8].wait()
        local[9].wait()
        for half in range(2):
            kw16[half] = kw[half].astype(BF16)
        k_copy.start()

    def upper_forward(r):
        def one(j, _):
            rcopy(
                gup.at[r, c, rows_of(j)], gup.at[r, c, rows_of(j)], up_s.at[r, j], up_r.at[r, j], partner
            ).wait_recv()
            rcopy(
                gup.at[r, c, rows_of(j)], gup.at[r, c, rows_of(j)], upc_s.at[r, j], upc_r.at[r, j], partner
            ).start()
            return 0

        lax.fori_loop(0, NX, one, 0)

    def upper_update(r):
        def wait(j):
            rcopy(
                gup.at[r, c, rows_of(j)], gup.at[r, other, rows_of(j)], upc_s.at[r, j], upc_r.at[r, j], partner
            ).wait_recv()

        @pl.when(r == 0)
        def _():
            def one(j, _):
                wait(j)
                for half in range(2):
                    got = gup[0, half, rows_of(j)]
                    tub[rows_of(j), half * HALF : (half + 1) * HALF] = got
                    tu[half, rows_of(j)] = got.astype(F32)
                    xu[half, rows_of(j)] = jnp.zeros((Q, HALF), F32)
                    hu[half, rows_of(j)] = jnp.zeros((Q, HALF), F32)
                return 0

            lax.fori_loop(0, NX, one, 0)

        @pl.when(r == 1)
        def _():
            rcopy(kup.at[other], kup.at[other], k_s.at[1], k_r.at[1], partner).wait_recv()

        @pl.when(r > 0)
        def _():
            a0, d0, ritz = coef[0], coef[1], coef[2]

            def one(j, _):
                wait(j)
                for half in range(2):
                    new_x = a0 * xu[half, rows_of(j)] + d0 * tu[half, rows_of(j)]
                    new_h = a0 * hu[half, rows_of(j)] + d0 * gup[r, half, rows_of(j)].astype(F32)
                    new_t = kup[half, rows_of(j)].astype(F32) * (new_h - ritz * new_x)
                    xu[half, rows_of(j)] = new_x
                    hu[half, rows_of(j)] = new_h
                    tu[half, rows_of(j)] = new_t
                    tub[rows_of(j), half * HALF : (half + 1) * HALF] = new_t.astype(BF16)
                return 0

            lax.fori_loop(0, NX, one, 0)

    def local_sums(extra):
        xb, tv, hb = x[c, rows_of(px)], t[c, rows_of(px)], h[c, rows_of(px)]
        return jnp.concatenate(
            [
                fold(xb * tv), fold(tv * tv), fold(tv * hb), extra,
                fold(xb * xb), fold(xb * hb), jnp.zeros((2, 128), F32),
            ],
            axis=0,
        )

    def stage(buf, ssem, rsem, size, me, dev_of):
        def send(r, value):
            buf[r, me] = value
            for k in range(1, size):
                rcopy(
                    buf.at[r, me], buf.at[r, me], ssem.at[r, k], rsem.at[r, me], dev_of(lax.rem(me + k, size))
                ).start()

        def finish(r):
            for k in range(1, size):
                src = lax.rem(me + k, size)
                rcopy(buf.at[r, me], buf.at[r, src], ssem.at[r, k], rsem.at[r, src], dev_of(src)).wait_recv()
            total = buf[r, 0]
            for k in range(1, size):
                total = total + buf[r, k]
            return total

        def drain(r):
            for k in range(1, size):
                rcopy(
                    buf.at[r, me], buf.at[r, me], ssem.at[r, k], rsem.at[r, me], dev_of(lax.rem(me + k, size))
                ).wait_send()

        return send, finish, drain

    c_send, c_finish, c_drain = stage(sc_c, scc_s, scc_r, 2, c, lambda i: (px * 2 + i, s))
    x_send, x_finish, x_drain = stage(sc_x, scx_s, scx_r, NX, px, lambda i: (i * 2 + c, s))
    y_send, y_finish, y_drain = stage(sc_y, scy_s, scy_r, ny, py, lambda i: (g, i * nz + pz))
    z_send, z_finish, z_drain = stage(sc_z, scz_s, scz_r, nz, pz, lambda i: (g, py * nz + i))

    def coefficients(total, r, ritz):
        sums = jnp.sum(total, axis=1, keepdims=True)
        xt, tt, th, tat, xx, xh = (sums[k : k + 1, 0:1] for k in range(6))
        norm = jnp.sqrt(tt)
        start = (jnp.zeros_like(norm), 1.0 / norm, tat / tt)
        n2 = tt - 2.0 * xt * xt + xt * xt * xx
        n = jnp.sqrt(n2)
        couple = (th - xt * xh) / n
        diag = (tat - 2.0 * xt * th + xt * xt * xh) / n2
        theta = (ritz + diag) / 2.0 - jnp.sqrt(((ritz - diag) / 2.0) ** 2 + couple**2)
        length = jnp.sqrt((diag - theta) ** 2 + couple**2)
        first = (diag - theta) / length
        second = -couple / length
        later = (first - second * xt / n, second / n, theta)
        return [jnp.where(r == 0, u, v) for u, v in zip(start, later)]

    def set_coef(total, r, ritz):
        a0, d0, new = coefficients(total, r, ritz)
        coef[0] = a0[0, 0]
        coef[1] = d0[0, 0]
        coef[2] = new[0, 0]
        return new

    def raise_inner():
        inner = dot(tb[...], rt[:, 0:512])
        in1[0:512] = inner[:, 0:256].astype(BF16)
        in1[512:1024] = inner[:, 256:512].astype(BF16)

    def round_body(r, ritz):
        @pl.when(r == 0)
        def _():
            ready_raise()

        raise_inner()
        praise[...] = dot(lr[...], in1[...])

        def raise_rows(k, _):
            j = xoff(k + 2)
            sr[r, rows_of(j)] = praise[rows_of(j)].astype(BF16)
            rcopy(sr.at[r, rows_of(j)], rr.at[r, rows_of(j)], sr_s.at[r, j], rr_r.at[r, j], (g, above)).start()
            return 0

        lax.fori_loop(0, NX, raise_rows, 0)

        @pl.when(r == 0)
        def _():
            ready_own()

        for k in range(4):
            inn[k * 512 : (k + 1) * 512] = dot(tb[...], rt[:, 512 + k * 256 : 768 + k * 256]).astype(BF16)
        upper_forward(r)
        acc[...] = dot(lo[:, 0:2048], inn[0:2048])

        def own_part(j, total):
            return total + fold(acc[rows_of(j)] * t[c, rows_of(j)])

        part = lax.fori_loop(0, NX, own_part, jnp.zeros((1, 128), F32))

        @pl.when(r == 0)
        def _():
            ready_lower()

        upper_update(r)

        def raise_part(j, total):
            return total + 2.0 * fold(praise[rows_of(j)] * tu[c, rows_of(j)])

        part = lax.fori_loop(0, NX, raise_part, part)
        c_send(r, local_sums(part))

        @pl.when(r == 0)
        def _():
            ready_weights()

        for k in range(2):
            inn[2048 + k * 512 : 2560 + k * 512] = dot(tub[...], ru[:, k * 256 : (k + 1) * 256]).astype(BF16)
        acc[...] += dot(lo[:, 2048:3072], inn[2048:3072])
        x_send(r, c_finish(r))

        def send_rows(k, _):
            j = xoff(k + 2)
            rcopy(sr.at[r, rows_of(j)], rr.at[r, rows_of(j)], sr_s.at[r, j], rr_r.at[r, j], (g, above)).wait_recv()
            value = acc[rows_of(j)] + rr[r, rows_of(j)].astype(F32)

            @pl.when(j == px)
            def _():
                keep_own[...] = value

            @pl.when(j != px)
            def _():
                so[r, rows_of(j)] = value.astype(BF16)
                rcopy(so.at[r, rows_of(j)], ro.at[r, px], so_s.at[r, j], ro_r.at[r, px], xdev(j, s)).start()

            return 0

        lax.fori_loop(0, NX, send_rows, 0)

        def own_in(k, _):
            j = xoff(k)
            rcopy(so.at[r, rows_of(j)], ro.at[r, j], so_s.at[r, j], ro_r.at[r, j], xdev(j, s)).wait_recv()
            return 0

        y_send(r, x_finish(r))
        lax.fori_loop(1, NX, own_in, 0)
        value = keep_own[...]
        for k in range(1, NX):
            value = value + ro[r, xoff(k)].astype(F32)
        block = (value * mask_of(px, c)).astype(BF16)
        gown[r, c, rows_of(px)] = block

        home = gown.at[r, c, rows_of(px)]
        rcopy(home, home, ownc_s.at[r, px], ownc_r.at[r, px], partner).start()
        for k in (2, 1, 3):
            j = xoff(k)
            rcopy(home, home, own_s.at[r, k], own_r.at[r, px], xdev(j, s)).start()
        rcopy(home, gup.at[r + 1, c, rows_of(px)], up_s.at[r + 1, px], up_r.at[r + 1, px], (g, below)).start()

        @pl.when(r == 0)
        def _():
            k_copy.wait_recv()
            k_forward.start()

        z_send(r, y_finish(r))

        for k in (1, 3, 2):
            j = xoff(k)
            there = gown.at[r, c, rows_of(j)]
            rcopy(there, there, own_s.at[r, k], own_r.at[r, j], partner).wait_recv()
            rcopy(there, there, ownc_s.at[r, j], ownc_r.at[r, j], partner).start()
            rcopy(there, gup.at[r + 1, c, rows_of(j)], up_s.at[r + 1, j], up_r.at[r + 1, j], (g, below)).start()

        new_ritz = set_coef(z_finish(r), r, ritz)

        @pl.when(r > 0)
        def _():
            energies[r - 1] = coef[2]

        a0, d0, theta = coef[0], coef[1], coef[2]

        def update(k, _):
            j = xoff(k)
            there = gown.at[r, other, rows_of(j)]
            rcopy(there, there, ownc_s.at[r, j], ownc_r.at[r, j], partner).wait_recv()
            for half in range(2):
                new_x = a0 * x[half, rows_of(j)] + d0 * t[half, rows_of(j)]
                new_h = a0 * h[half, rows_of(j)] + d0 * gown[r, half, rows_of(j)].astype(F32)
                new_t = kw[half, rows_of(j)] * (new_h - theta * new_x)
                x[half, rows_of(j)] = new_x
                h[half, rows_of(j)] = new_h
                t[half, rows_of(j)] = new_t
                tb[rows_of(j), half * HALF : (half + 1) * HALF] = new_t.astype(BF16)
            return 0

        lax.fori_loop(0, NX, update, 0)
        return new_ritz

    ritz = lax.fori_loop(0, ITERS, round_body, jnp.zeros((1, 1), F32))

    last = ITERS
    raise_inner()
    inn[0:512] = dot(tb[...], rt[:, 512:768]).astype(BF16)
    inn[512:1024] = dot(tb[...], rt[:, 768:1024]).astype(BF16)

    upper_forward(last)
    praise[...] = dot(lr[...], in1[...])
    acc[...] = dot(lo[:, 0:1024], inn[0:1024])

    def last_own(j, part):
        return part + 2.0 * fold(acc[rows_of(j)] * t[c, rows_of(j)])

    part = lax.fori_loop(0, NX, last_own, jnp.zeros((1, 128), F32))
    upper_update(last)

    def last_part(j, total):
        return total + 2.0 * fold(praise[rows_of(j)] * tu[c, rows_of(j)])

    part = lax.fori_loop(0, NX, last_part, part)
    c_send(last, local_sums(part))
    x_send(last, c_finish(last))

    def drain_round(r, _):
        def rows(j, _):
            rcopy(sr.at[r, rows_of(j)], rr.at[r, rows_of(j)], sr_s.at[r, j], rr_r.at[r, j], (g, above)).wait_send()
            home = gown.at[r, c, rows_of(px)]
            rcopy(home, home, ownc_s.at[r, j], ownc_r.at[r, px], partner).wait_send()
            return 0

        def others(k, _):
            j = xoff(k)
            rcopy(so.at[r, rows_of(j)], ro.at[r, px], so_s.at[r, j], ro_r.at[r, px], xdev(j, s)).wait_send()
            home = gown.at[r, c, rows_of(px)]
            rcopy(home, home, own_s.at[r, k], own_r.at[r, px], xdev(j, s)).wait_send()
            return 0

        lax.fori_loop(0, NX, rows, 0)
        lax.fori_loop(1, NX, others, 0)
        return 0

    def drain_upper(r, _):
        def rows(j, _):
            there = gup.at[r, c, rows_of(j)]
            rcopy(there, there, up_s.at[r, j], up_r.at[r, j], (g, below)).wait_send()
            rcopy(there, there, upc_s.at[r, j], upc_r.at[r, j], partner).wait_send()
            return 0

        lax.fori_loop(0, NX, rows, 0)
        return 0

    lax.fori_loop(0, ITERS, drain_round, 0)
    lax.fori_loop(0, ITERS + 1, drain_upper, 0)
    for copy in env:
        copy.wait_send()
    k_copy.wait_send()
    k_forward.wait_send()

    y_send(last, x_finish(last))
    z_send(last, y_finish(last))
    set_coef(z_finish(last), last, ritz)
    energies[last - 1] = coef[2]
    a0, d0 = coef[0], coef[1]

    def write(j, _):
        for half in range(2):
            out[rows_of(j), half * HALF : (half + 1) * HALF] = a0 * x[half, rows_of(j)] + d0 * t[half, rows_of(j)]
        return 0

    lax.fori_loop(0, NX, write, 0)

    def drain_sums(r, _):
        for drain in (c_drain, x_drain, y_drain, z_drain):
            drain(r)
        return 0

    lax.fori_loop(0, ITERS + 1, drain_sums, 0)


def body(left_env, right_env, guess, precond, sector_rows):
    sectors = lax.axis_size("sec")
    ny = min(NY, sectors)
    nz = sectors // ny
    rounds = ITERS + 1
    vm, dma = pltpu.VMEM, pltpu.SemaphoreType.DMA
    halves = (2, B, HALF)
    scratch = [
        vm((B, 1024), BF16), vm((B, 3072), BF16), vm((B, 1536), BF16), vm((B, 512), BF16), vm((4, HALF, B), BF16),
        vm(halves, F32), vm(halves, BF16), vm(halves, BF16), vm(halves, BF16),
        vm(halves, F32), vm(halves, F32), vm(halves, F32), vm(halves, F32), vm(halves, F32), vm(halves, F32),
        vm((B, B), BF16), vm((B, B), BF16),
        vm((ITERS,) + halves, BF16), vm((rounds,) + halves, BF16),
        vm((ITERS, B, HALF), BF16), vm((ITERS, B, HALF), BF16),
        vm((ITERS, NX, Q, HALF), BF16), vm((ITERS, B, HALF), BF16),
        vm((B, HALF), F32), vm((B, HALF), F32), vm((1024, HALF), BF16), vm((3072, HALF), BF16), vm((Q, HALF), F32),
        vm((rounds, 2, 8, 128), F32), vm((rounds, NX, 8, 128), F32),
        vm((rounds, ny, 8, 128), F32), vm((rounds, nz, 8, 128), F32),
        pltpu.SMEM((4,), F32),
        dma((10,)), dma((6,)), dma((6,)), dma((2,)), dma((2,)),
        dma((rounds, NX)), dma((rounds, NX)), dma((rounds, NX)), dma((rounds, NX)),
        dma((ITERS, NX)), dma((ITERS, NX)), dma((ITERS, NX)), dma((ITERS, NX)),
        dma((ITERS, NX)), dma((ITERS, NX)), dma((ITERS, NX)), dma((ITERS, NX)),
        dma((rounds, 2)), dma((rounds, 2)), dma((rounds, NX)), dma((rounds, NX)),
        dma((rounds, ny)), dma((rounds, ny)), dma((rounds, nz)), dma((rounds, nz)),
    ]
    any_space = pl.BlockSpec(memory_space=pl.ANY)
    vector, energies = pl.pallas_call(
        functools.partial(kernel, sectors, ny, nz),
        out_shape=(jax.ShapeDtypeStruct((B, B), F32), jax.ShapeDtypeStruct((ITERS,), F32)),
        in_specs=[any_space] * 4 + [pl.BlockSpec(memory_space=pltpu.SMEM)],
        out_specs=(pl.BlockSpec(memory_space=pltpu.VMEM), pl.BlockSpec(memory_space=pltpu.SMEM)),
        scratch_shapes=scratch,
        compiler_params=pltpu.CompilerParams(
            collective_id=0, has_side_effects=True, vmem_limit_bytes=56 * 1024 * 1024
        ),
        name="davidson",
    )(left_env, right_env, guess, precond, sector_rows)
    return vector * math.sqrt(float(B * B * sectors)), energies


def solution(mesh):
    in_specs = (
        P("grp", None, "sec", None),
        P("grp", None, "sec", None),
        P("sec", None),
        P("sec", None),
        P("sec"),
    )
    out_specs = (P("sec", None), P())
    return jax.shard_map(body, mesh=mesh, in_specs=in_specs, out_specs=out_specs, check_vma=False)
```

```python
import functools
import math

import jax
import jax.numpy as jnp
from jax import lax
from jax.experimental import pallas as pl
from jax.experimental.pallas import tpu as pltpu
from jax.sharding import PartitionSpec as P

ITERS = 3
B = 512
HALF = 256
Q = 128
NX = 4
NY = 4
MESH = pl.DeviceIdType.MESH
F32 = jnp.float32
BF16 = jnp.bfloat16


def rows_of(j):
    return pl.ds(pl.multiple_of(j * Q, Q), Q)


def dot(a, b):
    return jnp.dot(a, b, preferred_element_type=F32)


def fold(values):
    total = values[:, 0:128]
    for k in range(1, values.shape[1] // 128):
        total = total + values[:, k * 128 : (k + 1) * 128]
    return jnp.sum(total, axis=0, keepdims=True)


def kernel(
    sectors, ny, nz,
    left, right, guess, precond, used_ref,
    out, energies,
    lr, lo, rt, ru, rraw,
    kw, kw16, kup, xsend,
    x, h, t, xu, hu, tu, tb, tub,
    gown, gup, so, sr, ro, rr,
    acc, praise, in1, inn, keep_own, staged,
    sc_x, sc_y, sc_z, sc_t, coef,
    load_sem, env_s, env_r, k_s, k_r,
    up_s, up_r, upc_s, upc_r, own_s, own_r, ownc_s, ownc_r,
    so_s, ro_r, sr_s, rr_r,
    scx_s, scx_r, scy_s, scy_r, scz_s, scz_r, sct_s, sct_r,
):
    g = lax.axis_index("grp")
    s = lax.axis_index("sec")
    px, c = g // 2, g % 2
    py, pz = s // nz, s % nz
    above = lax.rem(s + 1, sectors)
    below = lax.rem(s + sectors - 1, sectors)
    other = 1 - c
    partner = (px * 2 + other, s)
    mine = pl.ds(pl.multiple_of(c * HALF, HALF), HALF)
    theirs = pl.ds(pl.multiple_of(other * HALF, HALF), HALF)

    def xdev(j, sec):
        return (j * 2 + c, sec)

    xs = [lax.rem(px + k, NX) for k in range(NX)]

    def xoff(k):
        return xs[k % NX]

    def rcopy(src, dst, ssem, rsem, dev):
        return pltpu.make_async_remote_copy(
            src_ref=src, dst_ref=dst, send_sem=ssem, recv_sem=rsem, device_id=dev, device_id_type=MESH
        )

    loads = [
        (right.at[0, 1, :, mine], rt.at[:, 0:256]),
        (left.at[0, 1], lr.at[:, 0:512]),
        (right.at[0, 0, :, mine], rt.at[:, 512:768]),
        (left.at[0, 0], lo.at[:, 0:512]),
        (right.at[0, 0, mine, :], rraw.at[0]),
        (right.at[0, 1, mine, :], rraw.at[2]),
        (guess.at[:, 0:256], t.at[0]),
        (guess.at[:, 256:512], t.at[1]),
        (precond.at[:, 0:256], kw.at[0]),
        (precond.at[:, 256:512], kw.at[1]),
    ]
    local = [pltpu.make_async_copy(a, b, load_sem.at[i]) for i, (a, b) in enumerate(loads)]
    for i in (6, 7, 1, 0, 3, 2, 4, 5, 8, 9):
        local[i].start()

    barrier = pltpu.get_barrier_semaphore()
    rows_y = [(px * 2 + 1, lax.rem(py + k, ny) * nz + pz) for k in range(1, ny)]
    column = [(px * 2 + 1, py * nz + lax.rem(pz + k, nz)) for k in range(1, nz)]
    shared = [partner]
    shared += [(xs[k] * 2 + core, s) for k in range(1, NX) for core in range(2)]
    shared += [(g, above), (g, below)]
    for peer in shared:
        pl.semaphore_signal(barrier, inc=1, device_id=peer, device_id_type=MESH)

    @pl.when(c == 1)
    def _():
        for peer in rows_y + column:
            pl.semaphore_signal(barrier, inc=1, device_id=peer, device_id_type=MESH)

    used = used_ref[0]
    row_ids = lax.broadcasted_iota(jnp.int32, (Q, HALF), 0)
    col_ids = lax.broadcasted_iota(jnp.int32, (Q, HALF), 1)

    def mask_of(j, half):
        return ((row_ids + j * Q < used) & (col_ids + half * HALF < used)).astype(F32)

    local[6].wait()
    local[7].wait()

    def start_rows(j, _):
        for half in range(2):
            value = t[half, rows_of(j)] * mask_of(j, half)
            t[half, rows_of(j)] = value
            x[half, rows_of(j)] = jnp.zeros((Q, HALF), F32)
            h[half, rows_of(j)] = jnp.zeros((Q, HALF), F32)
            rounded = value.astype(BF16)
            tb[rows_of(j), half * HALF : (half + 1) * HALF] = rounded
            xsend[half, rows_of(j)] = rounded
        return 0

    lax.fori_loop(0, NX, start_rows, 0)

    @pl.when(c == 1)
    def _():
        pl.semaphore_wait(barrier, len(shared + rows_y + column))

    @pl.when(c == 0)
    def _():
        pl.semaphore_wait(barrier, len(shared))


    for j in range(NX):
        rcopy(
            xsend.at[c, rows_of(j)], gup.at[0, c, rows_of(j)], up_s.at[0, j], up_r.at[0, j], (g, below)
        ).start()
    envs = [
        (left.at[0, 1], lr.at[:, 512:1024]),
        (right.at[0, 1, :, theirs], rt.at[:, 256:512]),
        (left.at[0, 0], lo.at[:, 512:1024]),
        (right.at[0, 0, :, theirs], rt.at[:, 768:1024]),
        (right.at[0, 0, theirs, :], rraw.at[1]),
        (right.at[0, 1, theirs, :], rraw.at[3]),
    ]
    env = [rcopy(a, b, env_s.at[i], env_r.at[i], partner) for i, (a, b) in enumerate(envs)]
    for copy in env:
        copy.start()

    k_copy = rcopy(kw16.at[c], kup.at[c], k_s.at[0], k_r.at[0], (g, below))
    k_forward = rcopy(kup.at[c], kup.at[c], k_s.at[1], k_r.at[1], partner)

    has_above = (s < sectors - 1).astype(F32)

    def gate(values):
        return (values.astype(F32) * has_above).astype(BF16)

    def ready_raise():
        local[0].wait()
        local[1].wait()
        env[0].wait_recv()
        env[1].wait_recv()
        rt[:, 0:512] = gate(rt[:, 0:512])

    def ready_own():
        for i in (2, 3, 4):
            local[i].wait()
        rt[:, 1024:1280] = rraw[0].T
        lo[:, 1024:1536] = lo[:, 0:512].T
        for i in (2, 3, 4):
            env[i].wait_recv()
        rt[:, 1280:1536] = rraw[1].T
        lo[:, 1536:2048] = lo[:, 512:1024].T

    def ready_lower():
        local[5].wait()
        ru[:, 0:256] = gate(rraw[2].T)
        lo[:, 2048:2560] = lr[:, 0:512].T
        env[5].wait_recv()
        ru[:, 256:512] = gate(rraw[3].T)
        lo[:, 2560:3072] = lr[:, 512:1024].T

    def ready_weights():
        local[8].wait()
        local[9].wait()
        for half in range(2):
            kw16[half] = kw[half].astype(BF16)
        k_copy.start()

    def upper_arrive(r, forward):
        for k in (0, 1, 3, 2):
            j = xoff(k)
            there = gup.at[r, c, rows_of(j)]
            rcopy(there, there, up_s.at[r, j], up_r.at[r, j], partner).wait_recv()
            if forward:
                rcopy(there, there, upc_s.at[r, j], upc_r.at[r, j], partner).start()

    def upper_wait(r, j):
        rcopy(
            gup.at[r, c, rows_of(j)], gup.at[r, other, rows_of(j)], upc_s.at[r, j], upc_r.at[r, j], partner
        ).wait_recv()

    def upper_half(r, half, exchanged):
        columns = slice(half * HALF, (half + 1) * HALF)

        @pl.when(r == 0)
        def _():
            for k in (0, 1, 3, 2):
                j = xoff(k)
                if exchanged:
                    upper_wait(r, j)
                got = gup[0, half, rows_of(j)]
                tub[rows_of(j), columns] = got
                tu[half, rows_of(j)] = got.astype(F32)
                xu[half, rows_of(j)] = jnp.zeros((Q, HALF), F32)
                hu[half, rows_of(j)] = jnp.zeros((Q, HALF), F32)

        @pl.when(r > 0)
        def _():
            a0, d0, ritz = coef[0], coef[1], coef[2]
            for k in (0, 1, 3, 2):
                j = xoff(k)
                if exchanged:
                    upper_wait(r, j)
                new_x = a0 * xu[half, rows_of(j)] + d0 * tu[half, rows_of(j)]
                new_h = a0 * hu[half, rows_of(j)] + d0 * gup[r, half, rows_of(j)].astype(F32)
                new_t = kup[half, rows_of(j)].astype(F32) * (new_h - ritz * new_x)
                xu[half, rows_of(j)] = new_x
                hu[half, rows_of(j)] = new_h
                tu[half, rows_of(j)] = new_t
                tub[rows_of(j), columns] = new_t.astype(BF16)

    def upper_own(r):
        for half in range(2):
            pl.when(c == half)(functools.partial(upper_half, r, half, False))

    def upper_other(r):
        @pl.when(r == 1)
        def _():
            rcopy(kup.at[other], kup.at[other], k_s.at[1], k_r.at[1], partner).wait_recv()

        for half in range(2):
            pl.when(other == half)(functools.partial(upper_half, r, half, True))

    def local_sums(extra):
        xb, tv, hb = x[c, rows_of(px)], t[c, rows_of(px)], h[c, rows_of(px)]
        return jnp.concatenate(
            [
                fold(xb * tv), fold(tv * tv), fold(tv * hb), extra,
                fold(xb * xb), fold(xb * hb), jnp.zeros((2, 128), F32),
            ],
            axis=0,
        )

    y_slots = [lax.rem(py + k, ny) for k in range(ny)]
    z_slots = [lax.rem(pz + k, nz) for k in range(nz)]
    my_slot = px * 2 + c

    def x_copy(r, k, slot):
        return rcopy(sc_x.at[r, slot], sc_x.at[r, slot], scx_s.at[r, k], scx_r.at[r, slot], (xs[k] * 2 + 1, s))

    def y_copy(r, k, slot):
        return rcopy(sc_y.at[r, slot], sc_y.at[r, slot], scy_s.at[r, k], scy_r.at[r, slot], rows_y[k - 1])

    def z_copy(r, k, slot):
        return rcopy(sc_z.at[r, slot], sc_z.at[r, slot], scz_s.at[r, k], scz_r.at[r, slot], column[k - 1])

    def t_copy(r):
        return rcopy(sc_t.at[r], sc_t.at[r], sct_s.at[r], sct_r.at[r], partner)

    def added(buf, r, size):
        total = buf[r, 0]
        for k in range(1, size):
            total = total + buf[r, k]
        return total

    def sums_out(r, value):
        sc_x[r, my_slot] = value
        for k in (2, 1, 3):
            x_copy(r, k, my_slot).start()

        @pl.when(c == 0)
        def _():
            x_copy(r, 0, my_slot).start()

    def rows_out(r):
        @pl.when(c == 1)
        def _():
            for k in range(NX):
                x_copy(r, k, xs[k] * 2).wait_recv()
                if k:
                    x_copy(r, k, xs[k] * 2 + 1).wait_recv()
            sc_y[r, py] = added(sc_x, r, 2 * NX)
            for k in range(1, ny):
                y_copy(r, k, py).start()

    def column_out(r):
        @pl.when(c == 1)
        def _():
            for k in range(1, ny):
                y_copy(r, k, y_slots[k]).wait_recv()
            sc_z[r, pz] = added(sc_y, r, ny)
            for k in range(1, nz):
                z_copy(r, k, pz).start()

    def total_out(r):
        @pl.when(c == 1)
        def _():
            for k in range(1, nz):
                z_copy(r, k, z_slots[k]).wait_recv()
            sc_t[r] = added(sc_z, r, nz)
            t_copy(r).start()

        @pl.when(c == 0)
        def _():
            t_copy(r).wait_recv()

        return sc_t[r]

    def sums_drain(r):
        for k in range(1, NX):
            x_copy(r, k, my_slot).wait_send()

        @pl.when(c == 0)
        def _():
            x_copy(r, 0, my_slot).wait_send()

        @pl.when(c == 1)
        def _():
            for k in range(1, ny):
                y_copy(r, k, py).wait_send()

    def column_drain(r):
        @pl.when(c == 1)
        def _():
            for k in range(1, nz):
                z_copy(r, k, pz).wait_send()
            t_copy(r).wait_send()

    def coefficients(total, r, ritz):
        sums = jnp.sum(total, axis=1, keepdims=True)
        xt, tt, th, tat, xx, xh = (sums[k : k + 1, 0:1] for k in range(6))
        norm = jnp.sqrt(tt)
        start = (jnp.zeros_like(norm), 1.0 / norm, tat / tt)
        n2 = tt - 2.0 * xt * xt + xt * xt * xx
        n = jnp.sqrt(n2)
        couple = (th - xt * xh) / n
        diag = (tat - 2.0 * xt * th + xt * xt * xh) / n2
        theta = (ritz + diag) / 2.0 - jnp.sqrt(((ritz - diag) / 2.0) ** 2 + couple**2)
        length = jnp.sqrt((diag - theta) ** 2 + couple**2)
        first = (diag - theta) / length
        second = -couple / length
        later = (first - second * xt / n, second / n, theta)
        return [jnp.where(r == 0, u, v) for u, v in zip(start, later)]

    def set_coef(total, r, ritz):
        a0, d0, new = coefficients(total, r, ritz)
        coef[0] = a0[0, 0]
        coef[1] = d0[0, 0]
        coef[2] = new[0, 0]
        return new

    def raise_inner():
        inner = dot(tb[...], rt[:, 0:512])
        in1[0:512] = inner[:, 0:256].astype(BF16)
        in1[512:1024] = inner[:, 256:512].astype(BF16)

    def round_body(r, ritz):
        @pl.when(r == 0)
        def _():
            ready_raise()

        raise_inner()
        praise[...] = dot(lr[...], in1[...])

        for k in (2, 3, 1, 0):
            j = xoff(k)
            sr[r, rows_of(j)] = praise[rows_of(j)].astype(BF16)
            rcopy(sr.at[r, rows_of(j)], rr.at[r, rows_of(j)], sr_s.at[r, j], rr_r.at[r, j], (g, above)).start()

        @pl.when(r == 0)
        def _():
            ready_own()
            ready_lower()

        for k in range(4):
            inn[k * 512 : (k + 1) * 512] = dot(tb[...], rt[:, 512 + k * 256 : 768 + k * 256]).astype(BF16)
        upper_arrive(r, True)
        acc[...] = dot(lo[:, 0:2048], inn[0:2048])

        def own_part(j, total):
            return total + fold(acc[rows_of(j)] * t[c, rows_of(j)])

        part = lax.fori_loop(0, NX, own_part, jnp.zeros((1, 128), F32))

        upper_own(r)

        def raise_part(j, total):
            return total + 2.0 * fold(praise[rows_of(j)] * tu[c, rows_of(j)])

        part = lax.fori_loop(0, NX, raise_part, part)
        sums_out(r, local_sums(part))
        upper_other(r)

        @pl.when(r == 0)
        def _():
            ready_weights()

        for k in range(2):
            inn[2048 + k * 512 : 2560 + k * 512] = dot(tub[...], ru[:, k * 256 : (k + 1) * 256]).astype(BF16)
        acc[...] += dot(lo[:, 2048:3072], inn[2048:3072])

        for k in (2, 3, 1, 0):
            if k == 0:
                rows_out(r)
            j = xoff(k)
            rcopy(sr.at[r, rows_of(j)], rr.at[r, rows_of(j)], sr_s.at[r, j], rr_r.at[r, j], (g, above)).wait_recv()
            value = acc[rows_of(j)] + rr[r, rows_of(j)].astype(F32)

            if k == 0:
                keep_own[...] = value
            else:
                so[r, rows_of(j)] = value.astype(BF16)
                rcopy(so.at[r, rows_of(j)], ro.at[r, px], so_s.at[r, j], ro_r.at[r, px], xdev(j, s)).start()

        column_out(r)
        for k in range(1, NX):
            j = xoff(k)
            rcopy(so.at[r, rows_of(j)], ro.at[r, j], so_s.at[r, j], ro_r.at[r, j], xdev(j, s)).wait_recv()
        value = keep_own[...]
        for k in range(1, NX):
            value = value + ro[r, xoff(k)].astype(F32)
        block = (value * mask_of(px, c)).astype(BF16)
        gown[r, c, rows_of(px)] = block

        home = gown.at[r, c, rows_of(px)]
        rcopy(home, home, ownc_s.at[r, px], ownc_r.at[r, px], partner).start()
        for k in (2, 1, 3):
            j = xoff(k)
            rcopy(home, home, own_s.at[r, k], own_r.at[r, px], xdev(j, s)).start()
        rcopy(home, gup.at[r + 1, c, rows_of(px)], up_s.at[r + 1, px], up_r.at[r + 1, px], (g, below)).start()

        @pl.when(r == 0)
        def _():
            k_copy.wait_recv()
            k_forward.start()


        for k in (1, 3, 2):
            j = xoff(k)
            there = gown.at[r, c, rows_of(j)]
            rcopy(there, there, own_s.at[r, k], own_r.at[r, j], partner).wait_recv()
            rcopy(there, there, ownc_s.at[r, j], ownc_r.at[r, j], partner).start()
            rcopy(there, gup.at[r + 1, c, rows_of(j)], up_s.at[r + 1, j], up_r.at[r + 1, j], (g, below)).start()

        new_ritz = set_coef(total_out(r), r, ritz)

        @pl.when(r > 0)
        def _():
            energies[r - 1] = coef[2]

        a0, d0, theta = coef[0], coef[1], coef[2]

        for k in range(NX):
            j = xoff(k)
            there = gown.at[r, other, rows_of(j)]
            rcopy(there, there, ownc_s.at[r, j], ownc_r.at[r, j], partner).wait_recv()
            for half in range(2):
                new_x = a0 * x[half, rows_of(j)] + d0 * t[half, rows_of(j)]
                new_h = a0 * h[half, rows_of(j)] + d0 * gown[r, half, rows_of(j)].astype(F32)
                new_t = kw[half, rows_of(j)] * (new_h - theta * new_x)
                x[half, rows_of(j)] = new_x
                h[half, rows_of(j)] = new_h
                t[half, rows_of(j)] = new_t
                tb[rows_of(j), half * HALF : (half + 1) * HALF] = new_t.astype(BF16)
        return new_ritz

    ritz = lax.fori_loop(0, ITERS, round_body, jnp.zeros((1, 1), F32))

    last = ITERS
    raise_inner()
    inn[0:512] = dot(tb[...], rt[:, 512:768]).astype(BF16)
    inn[512:1024] = dot(tb[...], rt[:, 768:1024]).astype(BF16)

    upper_arrive(last, False)
    praise[...] = dot(lr[...], in1[...])
    acc[...] = dot(lo[:, 0:1024], inn[0:1024])

    def last_own(j, part):
        return part + 2.0 * fold(acc[rows_of(j)] * t[c, rows_of(j)])

    part = lax.fori_loop(0, NX, last_own, jnp.zeros((1, 128), F32))
    upper_own(last)

    def last_part(j, total):
        return total + 2.0 * fold(praise[rows_of(j)] * tu[c, rows_of(j)])

    part = lax.fori_loop(0, NX, last_part, part)
    sums_out(last, local_sums(part))

    def drain_round(r, _):
        for j in range(NX):
            rcopy(sr.at[r, rows_of(j)], rr.at[r, rows_of(j)], sr_s.at[r, j], rr_r.at[r, j], (g, above)).wait_send()
            home = gown.at[r, c, rows_of(px)]
            rcopy(home, home, ownc_s.at[r, j], ownc_r.at[r, px], partner).wait_send()
        for k in range(1, NX):
            j = xoff(k)
            rcopy(so.at[r, rows_of(j)], ro.at[r, px], so_s.at[r, j], ro_r.at[r, px], xdev(j, s)).wait_send()
            rcopy(home, home, own_s.at[r, k], own_r.at[r, px], xdev(j, s)).wait_send()
        return 0

    def drain_upper(r, _):
        for j in range(NX):
            there = gup.at[r, c, rows_of(j)]
            rcopy(there, there, up_s.at[r, j], up_r.at[r, j], (g, below)).wait_send()

            @pl.when(r < ITERS)
            def _():
                rcopy(there, there, upc_s.at[r, j], upc_r.at[r, j], partner).wait_send()

        return 0

    def drain_sums(r, _):
        sums_drain(r)
        column_drain(r)
        return 0

    lax.fori_loop(0, ITERS, drain_round, 0)
    rows_out(last)
    lax.fori_loop(0, ITERS + 1, drain_upper, 0)
    for copy in env:
        copy.wait_send()
    k_copy.wait_send()
    k_forward.wait_send()

    column_out(last)
    lax.fori_loop(0, ITERS, drain_sums, 0)
    sums_drain(last)
    set_coef(total_out(last), last, ritz)
    energies[last - 1] = coef[2]
    a0, d0 = coef[0], coef[1]

    writes = []
    for j in range(NX):
        for half in range(2):
            staged[rows_of(j), half * HALF : (half + 1) * HALF] = (
                a0 * x[half, rows_of(j)] + d0 * t[half, rows_of(j)]
            )
        writes.append(pltpu.make_async_copy(staged.at[rows_of(j)], out.at[rows_of(j)], load_sem.at[j]))
        writes[-1].start()

    column_drain(last)
    for copy in writes:
        copy.wait()


def body(left_env, right_env, guess, precond, sector_rows):
    sectors = lax.axis_size("sec")
    ny = min(NY, sectors)
    nz = sectors // ny
    rounds = ITERS + 1
    vm, dma = pltpu.VMEM, pltpu.SemaphoreType.DMA
    halves = (2, B, HALF)
    scratch = [
        vm((B, 1024), BF16), vm((B, 3072), BF16), vm((B, 1536), BF16), vm((B, 512), BF16), vm((4, HALF, B), BF16),
        vm(halves, F32), vm(halves, BF16), vm(halves, BF16), vm(halves, BF16),
        vm(halves, F32), vm(halves, F32), vm(halves, F32), vm(halves, F32), vm(halves, F32), vm(halves, F32),
        vm((B, B), BF16), vm((B, B), BF16),
        vm((ITERS,) + halves, BF16), vm((rounds,) + halves, BF16),
        vm((ITERS, B, HALF), BF16), vm((ITERS, B, HALF), BF16),
        vm((ITERS, NX, Q, HALF), BF16), vm((ITERS, B, HALF), BF16),
        vm((B, HALF), F32), vm((B, HALF), F32), vm((1024, HALF), BF16), vm((3072, HALF), BF16), vm((Q, HALF), F32), vm((B, B), F32),
        vm((rounds, 2 * NX, 8, 128), F32), vm((rounds, ny, 8, 128), F32),
        vm((rounds, nz, 8, 128), F32), vm((rounds, 8, 128), F32),
        pltpu.SMEM((4,), F32),
        dma((10,)), dma((6,)), dma((6,)), dma((2,)), dma((2,)),
        dma((rounds, NX)), dma((rounds, NX)), dma((rounds, NX)), dma((rounds, NX)),
        dma((ITERS, NX)), dma((ITERS, NX)), dma((ITERS, NX)), dma((ITERS, NX)),
        dma((ITERS, NX)), dma((ITERS, NX)), dma((ITERS, NX)), dma((ITERS, NX)),
        dma((rounds, NX)), dma((rounds, 2 * NX)), dma((rounds, ny)), dma((rounds, ny)),
        dma((rounds, nz)), dma((rounds, nz)), dma((rounds,)), dma((rounds,)),
    ]
    any_space = pl.BlockSpec(memory_space=pl.ANY)
    vector, energies = pl.pallas_call(
        functools.partial(kernel, sectors, ny, nz),
        out_shape=(jax.ShapeDtypeStruct((B, B), F32), jax.ShapeDtypeStruct((ITERS,), F32)),
        in_specs=[any_space] * 4 + [pl.BlockSpec(memory_space=pltpu.SMEM)],
        out_specs=(pl.BlockSpec(memory_space=pl.ANY), pl.BlockSpec(memory_space=pltpu.SMEM)),
        scratch_shapes=scratch,
        compiler_params=pltpu.CompilerParams(
            collective_id=0, has_side_effects=True, vmem_limit_bytes=56 * 1024 * 1024
        ),
        name="davidson",
    )(left_env, right_env, guess, precond, sector_rows)
    return vector * math.sqrt(float(B * B * sectors)), energies


def solution(mesh):
    in_specs = (
        P("grp", None, "sec", None),
        P("grp", None, "sec", None),
        P("sec", None),
        P("sec", None),
        P("sec"),
    )
    out_specs = (P("sec", None), P())
    return jax.shard_map(body, mesh=mesh, in_specs=in_specs, out_specs=out_specs, check_vma=False)
```

```python
import functools
import math

import jax
import jax.numpy as jnp
from jax import lax
from jax.experimental import pallas as pl
from jax.experimental.pallas import tpu as pltpu
from jax.sharding import PartitionSpec as P

ITERS = 3
B = 512
HALF = 256
Q = 128
NX = 4
NY = 4
MESH = pl.DeviceIdType.MESH
F32 = jnp.float32
BF16 = jnp.bfloat16


def rows_of(j):
    return pl.ds(pl.multiple_of(j * Q, Q), Q)


def dot(a, b):
    return jnp.dot(a, b, preferred_element_type=F32)


def fold(values):
    total = values[:, 0:128]
    for k in range(1, values.shape[1] // 128):
        total = total + values[:, k * 128 : (k + 1) * 128]
    return jnp.sum(total, axis=0, keepdims=True)


def kernel(
    sectors, ny, nz,
    left, right, guess, precond, used_ref,
    out, energies,
    lr, lo, rt, ru, rraw,
    kw, kw16, kup, xsend,
    x, h, t, xu, hu, tu, tb, tub,
    gown, gup, so, sr, ro, rr,
    acc, praise, in1, inn, keep_own, staged,
    sc_x, sc_y, sc_z, sc_t, coef,
    load_sem, env_s, env_r, k_s, k_r,
    up_s, up_r, upc_s, upc_r, own_s, own_r, ownc_s, ownc_r,
    so_s, ro_r, sr_s, rr_r,
    scx_s, scx_r, scy_s, scy_r, scz_s, scz_r, sct_s, sct_r,
):
    g = lax.axis_index("grp")
    s = lax.axis_index("sec")
    px, c = g // 2, g % 2
    py, pz = s // nz, s % nz
    above = lax.rem(s + 1, sectors)
    below = lax.rem(s + sectors - 1, sectors)
    other = 1 - c
    partner = (px * 2 + other, s)
    mine = pl.ds(pl.multiple_of(c * HALF, HALF), HALF)
    theirs = pl.ds(pl.multiple_of(other * HALF, HALF), HALF)

    def xdev(j, sec):
        return (j * 2 + c, sec)

    xs = [lax.rem(px + k, NX) for k in range(NX)]

    def xoff(k):
        return xs[k % NX]

    def rcopy(src, dst, ssem, rsem, dev):
        return pltpu.make_async_remote_copy(
            src_ref=src, dst_ref=dst, send_sem=ssem, recv_sem=rsem, device_id=dev, device_id_type=MESH
        )

    loads = [
        (right.at[0, 1, :, mine], rt.at[:, 0:256]),
        (left.at[0, 1], lr.at[:, 0:512]),
        (right.at[0, 0, :, mine], rt.at[:, 512:768]),
        (left.at[0, 0], lo.at[:, 0:512]),
        (right.at[0, 0, mine, :], rraw.at[0]),
        (right.at[0, 1, mine, :], rraw.at[2]),
        (guess.at[:, 0:256], t.at[0]),
        (guess.at[:, 256:512], t.at[1]),
        (precond.at[:, 0:256], kw.at[0]),
        (precond.at[:, 256:512], kw.at[1]),
    ]
    local = [pltpu.make_async_copy(a, b, load_sem.at[i]) for i, (a, b) in enumerate(loads)]
    for i in (6, 7, 1, 0, 3, 2, 4, 5, 8, 9):
        local[i].start()

    barrier = pltpu.get_barrier_semaphore()
    rows_y = [(px * 2 + 1, lax.rem(py + k, ny) * nz + pz) for k in range(1, ny)]
    column = [(px * 2 + 1, py * nz + lax.rem(pz + k, nz)) for k in range(1, nz)]
    shared = [partner]
    shared += [(xs[k] * 2 + core, s) for k in range(1, NX) for core in range(2)]
    shared += [(g, above), (g, below)]
    for peer in shared:
        pl.semaphore_signal(barrier, inc=1, device_id=peer, device_id_type=MESH)

    @pl.when(c == 1)
    def _():
        for peer in rows_y + column:
            pl.semaphore_signal(barrier, inc=1, device_id=peer, device_id_type=MESH)

    used = used_ref[0]
    row_ids = lax.broadcasted_iota(jnp.int32, (Q, HALF), 0)
    col_ids = lax.broadcasted_iota(jnp.int32, (Q, HALF), 1)

    def mask_of(j, half):
        return ((row_ids + j * Q < used) & (col_ids + half * HALF < used)).astype(F32)

    local[6].wait()
    local[7].wait()

    def start_rows(j, _):
        for half in range(2):
            value = t[half, rows_of(j)] * mask_of(j, half)
            t[half, rows_of(j)] = value
            x[half, rows_of(j)] = jnp.zeros((Q, HALF), F32)
            h[half, rows_of(j)] = jnp.zeros((Q, HALF), F32)
            rounded = value.astype(BF16)
            tb[rows_of(j), half * HALF : (half + 1) * HALF] = rounded
            xsend[half, rows_of(j)] = rounded
        return 0

    lax.fori_loop(0, NX, start_rows, 0)

    @pl.when(c == 1)
    def _():
        pl.semaphore_wait(barrier, len(shared + rows_y + column))

    @pl.when(c == 0)
    def _():
        pl.semaphore_wait(barrier, len(shared))


    for j in range(NX):
        rcopy(
            xsend.at[c, rows_of(j)], gup.at[0, c, rows_of(j)], up_s.at[0, j], up_r.at[0, j], (g, below)
        ).start()
    envs = [
        (left.at[0, 1], lr.at[:, 512:1024]),
        (right.at[0, 1, :, theirs], rt.at[:, 256:512]),
        (left.at[0, 0], lo.at[:, 512:1024]),
        (right.at[0, 0, :, theirs], rt.at[:, 768:1024]),
        (right.at[0, 0, theirs, :], rraw.at[1]),
        (right.at[0, 1, theirs, :], rraw.at[3]),
    ]
    env = [rcopy(a, b, env_s.at[i], env_r.at[i], partner) for i, (a, b) in enumerate(envs)]
    for copy in env:
        copy.start()

    k_copy = rcopy(kw16.at[c], kup.at[c], k_s.at[0], k_r.at[0], (g, below))
    k_forward = rcopy(kup.at[c], kup.at[c], k_s.at[1], k_r.at[1], partner)

    has_above = (s < sectors - 1).astype(F32)

    def gate(values):
        return (values.astype(F32) * has_above).astype(BF16)

    def ready_raise():
        local[0].wait()
        local[1].wait()
        env[0].wait_recv()
        env[1].wait_recv()
        rt[:, 0:512] = gate(rt[:, 0:512])

    def ready_own():
        for i in (2, 3, 4):
            local[i].wait()
        rt[:, 1024:1280] = rraw[0].T
        lo[:, 1024:1536] = lo[:, 0:512].T
        for i in (2, 3, 4):
            env[i].wait_recv()
        rt[:, 1280:1536] = rraw[1].T
        lo[:, 1536:2048] = lo[:, 512:1024].T

    def ready_lower():
        local[5].wait()
        ru[:, 0:256] = gate(rraw[2].T)
        lo[:, 2048:2560] = lr[:, 0:512].T
        env[5].wait_recv()
        ru[:, 256:512] = gate(rraw[3].T)
        lo[:, 2560:3072] = lr[:, 512:1024].T

    def ready_weights():
        local[8].wait()
        local[9].wait()
        for half in range(2):
            kw16[half] = kw[half].astype(BF16)
        k_copy.start()

    def upper_arrive(r, forward):
        for k in (0, 1, 3, 2):
            j = xoff(k)
            there = gup.at[r, c, rows_of(j)]
            rcopy(there, there, up_s.at[r, j], up_r.at[r, j], partner).wait_recv()
            if forward:
                rcopy(there, there, upc_s.at[r, j], upc_r.at[r, j], partner).start()

    def upper_wait(r, j):
        rcopy(
            gup.at[r, c, rows_of(j)], gup.at[r, other, rows_of(j)], upc_s.at[r, j], upc_r.at[r, j], partner
        ).wait_recv()

    def upper_half(r, half, exchanged):
        columns = slice(half * HALF, (half + 1) * HALF)

        @pl.when(r == 0)
        def _():
            for k in (0, 1, 3, 2):
                j = xoff(k)
                if exchanged:
                    upper_wait(r, j)
                got = gup[0, half, rows_of(j)]
                tub[rows_of(j), columns] = got
                tu[half, rows_of(j)] = got.astype(F32)
                xu[half, rows_of(j)] = jnp.zeros((Q, HALF), F32)
                hu[half, rows_of(j)] = jnp.zeros((Q, HALF), F32)

        @pl.when(r > 0)
        def _():
            a0, d0, ritz = coef[0], coef[1], coef[2]
            for k in (0, 1, 3, 2):
                j = xoff(k)
                if exchanged:
                    upper_wait(r, j)
                new_x = a0 * xu[half, rows_of(j)] + d0 * tu[half, rows_of(j)]
                new_h = a0 * hu[half, rows_of(j)] + d0 * gup[r, half, rows_of(j)].astype(F32)
                new_t = kup[half, rows_of(j)].astype(F32) * (new_h - ritz * new_x)
                xu[half, rows_of(j)] = new_x
                hu[half, rows_of(j)] = new_h
                tu[half, rows_of(j)] = new_t
                tub[rows_of(j), columns] = new_t.astype(BF16)

    def upper_own(r):
        for half in range(2):
            pl.when(c == half)(functools.partial(upper_half, r, half, False))

    def upper_other(r):
        @pl.when(r == 1)
        def _():
            rcopy(kup.at[other], kup.at[other], k_s.at[1], k_r.at[1], partner).wait_recv()

        for half in range(2):
            pl.when(other == half)(functools.partial(upper_half, r, half, True))

    def local_sums(extra):
        xb, tv, hb = x[c, rows_of(px)], t[c, rows_of(px)], h[c, rows_of(px)]
        return jnp.concatenate(
            [
                fold(xb * tv), fold(tv * tv), fold(tv * hb), extra,
                fold(xb * xb), fold(xb * hb), jnp.zeros((2, 128), F32),
            ],
            axis=0,
        )

    y_slots = [lax.rem(py + k, ny) for k in range(ny)]
    z_slots = [lax.rem(pz + k, nz) for k in range(nz)]
    my_slot = px * 2 + c

    def x_copy(r, k, slot):
        return rcopy(sc_x.at[r, slot], sc_x.at[r, slot], scx_s.at[r, k], scx_r.at[r, slot], (xs[k] * 2 + 1, s))

    def y_copy(r, k, slot):
        return rcopy(sc_y.at[r, slot], sc_y.at[r, slot], scy_s.at[r, k], scy_r.at[r, slot], rows_y[k - 1])

    def z_copy(r, k, slot):
        return rcopy(sc_z.at[r, slot], sc_z.at[r, slot], scz_s.at[r, k], scz_r.at[r, slot], column[k - 1])

    def t_copy(r):
        return rcopy(sc_t.at[r], sc_t.at[r], sct_s.at[r], sct_r.at[r], partner)

    def added(buf, r, size):
        total = buf[r, 0]
        for k in range(1, size):
            total = total + buf[r, k]
        return total

    def sums_out(r, value):
        sc_x[r, my_slot] = value
        for k in (2, 1, 3):
            x_copy(r, k, my_slot).start()

        @pl.when(c == 0)
        def _():
            x_copy(r, 0, my_slot).start()

    def rows_out(r):
        @pl.when(c == 1)
        def _():
            for k in range(NX):
                x_copy(r, k, xs[k] * 2).wait_recv()
                if k:
                    x_copy(r, k, xs[k] * 2 + 1).wait_recv()
            sc_y[r, py] = added(sc_x, r, 2 * NX)
            for k in sorted(range(1, ny), key=lambda k: -min(k, ny - k)):
                y_copy(r, k, py).start()

    def column_out(r):
        @pl.when(c == 1)
        def _():
            for k in range(1, ny):
                y_copy(r, k, y_slots[k]).wait_recv()
            sc_z[r, pz] = added(sc_y, r, ny)
            for k in sorted(range(1, nz), key=lambda k: -min(k, nz - k)):
                z_copy(r, k, pz).start()

    def total_out(r):
        @pl.when(c == 1)
        def _():
            for k in range(1, nz):
                z_copy(r, k, z_slots[k]).wait_recv()
            sc_t[r] = added(sc_z, r, nz)
            t_copy(r).start()

        @pl.when(c == 0)
        def _():
            t_copy(r).wait_recv()

        return sc_t[r]

    def sums_drain(r):
        for k in range(1, NX):
            x_copy(r, k, my_slot).wait_send()

        @pl.when(c == 0)
        def _():
            x_copy(r, 0, my_slot).wait_send()

        @pl.when(c == 1)
        def _():
            for k in range(1, ny):
                y_copy(r, k, py).wait_send()

    def column_drain(r):
        @pl.when(c == 1)
        def _():
            for k in range(1, nz):
                z_copy(r, k, pz).wait_send()
            t_copy(r).wait_send()

    def coefficients(total, r, ritz):
        sums = jnp.sum(total, axis=1, keepdims=True)
        xt, tt, th, tat, xx, xh = (sums[k : k + 1, 0:1] for k in range(6))
        norm = jnp.sqrt(tt)
        start = (jnp.zeros_like(norm), 1.0 / norm, tat / tt)
        n2 = tt - 2.0 * xt * xt + xt * xt * xx
        n = jnp.sqrt(n2)
        couple = (th - xt * xh) / n
        diag = (tat - 2.0 * xt * th + xt * xt * xh) / n2
        theta = (ritz + diag) / 2.0 - jnp.sqrt(((ritz - diag) / 2.0) ** 2 + couple**2)
        length = jnp.sqrt((diag - theta) ** 2 + couple**2)
        first = (diag - theta) / length
        second = -couple / length
        later = (first - second * xt / n, second / n, theta)
        return [jnp.where(r == 0, u, v) for u, v in zip(start, later)]

    def set_coef(total, r, ritz):
        a0, d0, new = coefficients(total, r, ritz)
        coef[0] = a0[0, 0]
        coef[1] = d0[0, 0]
        coef[2] = new[0, 0]
        return new

    def raise_inner():
        inner = dot(tb[...], rt[:, 0:512])
        in1[0:512] = inner[:, 0:256].astype(BF16)
        in1[512:1024] = inner[:, 256:512].astype(BF16)

    def round_body(r, ritz):
        @pl.when(r == 0)
        def _():
            ready_raise()

        raise_inner()
        praise[...] = dot(lr[...], in1[...])

        for k in (2, 3, 1, 0):
            j = xoff(k)
            sr[r, rows_of(j)] = praise[rows_of(j)].astype(BF16)
            rcopy(sr.at[r, rows_of(j)], rr.at[r, rows_of(j)], sr_s.at[r, j], rr_r.at[r, j], (g, above)).start()

        @pl.when(r == 0)
        def _():
            ready_own()
            ready_lower()

        for k in range(4):
            inn[k * 512 : (k + 1) * 512] = dot(tb[...], rt[:, 512 + k * 256 : 768 + k * 256]).astype(BF16)
        pl.when(c == 1)(functools.partial(upper_arrive, r, True))
        acc[...] = dot(lo[:, 0:2048], inn[0:2048])

        pl.when(c == 0)(functools.partial(upper_arrive, r, True))

        def own_part(j, total):
            return total + fold(acc[rows_of(j)] * t[c, rows_of(j)])

        part = lax.fori_loop(0, NX, own_part, jnp.zeros((1, 128), F32))

        upper_own(r)

        def raise_part(j, total):
            return total + 2.0 * fold(praise[rows_of(j)] * tu[c, rows_of(j)])

        part = lax.fori_loop(0, NX, raise_part, part)
        sums_out(r, local_sums(part))
        upper_other(r)

        @pl.when(r == 0)
        def _():
            ready_weights()

        for k in range(2):
            inn[2048 + k * 512 : 2560 + k * 512] = dot(tub[...], ru[:, k * 256 : (k + 1) * 256]).astype(BF16)
        acc[...] += dot(lo[:, 2048:3072], inn[2048:3072])

        for k in (2, 3, 1, 0):
            if k == 0:
                rows_out(r)
            j = xoff(k)
            rcopy(sr.at[r, rows_of(j)], rr.at[r, rows_of(j)], sr_s.at[r, j], rr_r.at[r, j], (g, above)).wait_recv()
            value = acc[rows_of(j)] + rr[r, rows_of(j)].astype(F32)

            if k == 0:
                keep_own[...] = value
            else:
                so[r, rows_of(j)] = value.astype(BF16)
                rcopy(so.at[r, rows_of(j)], ro.at[r, px], so_s.at[r, j], ro_r.at[r, px], xdev(j, s)).start()

        column_out(r)
        for k in range(1, NX):
            j = xoff(k)
            rcopy(so.at[r, rows_of(j)], ro.at[r, j], so_s.at[r, j], ro_r.at[r, j], xdev(j, s)).wait_recv()
        value = keep_own[...]
        for k in range(1, NX):
            value = value + ro[r, xoff(k)].astype(F32)
        block = (value * mask_of(px, c)).astype(BF16)
        gown[r, c, rows_of(px)] = block

        home = gown.at[r, c, rows_of(px)]
        rcopy(home, home, ownc_s.at[r, px], ownc_r.at[r, px], partner).start()
        for k in (2, 1, 3):
            j = xoff(k)
            rcopy(home, home, own_s.at[r, k], own_r.at[r, px], xdev(j, s)).start()
        rcopy(home, gup.at[r + 1, c, rows_of(px)], up_s.at[r + 1, px], up_r.at[r + 1, px], (g, below)).start()

        @pl.when(r == 0)
        def _():
            k_copy.wait_recv()
            k_forward.start()


        for k in (1, 3, 2):
            j = xoff(k)
            there = gown.at[r, c, rows_of(j)]
            rcopy(there, there, own_s.at[r, k], own_r.at[r, j], partner).wait_recv()
            rcopy(there, there, ownc_s.at[r, j], ownc_r.at[r, j], partner).start()
            rcopy(there, gup.at[r + 1, c, rows_of(j)], up_s.at[r + 1, j], up_r.at[r + 1, j], (g, below)).start()

        new_ritz = set_coef(total_out(r), r, ritz)

        @pl.when(r > 0)
        def _():
            energies[r - 1] = coef[2]

        a0, d0, theta = coef[0], coef[1], coef[2]

        for k in range(NX):
            j = xoff(k)
            there = gown.at[r, other, rows_of(j)]
            rcopy(there, there, ownc_s.at[r, j], ownc_r.at[r, j], partner).wait_recv()
            for half in range(2):
                new_x = a0 * x[half, rows_of(j)] + d0 * t[half, rows_of(j)]
                new_h = a0 * h[half, rows_of(j)] + d0 * gown[r, half, rows_of(j)].astype(F32)
                new_t = kw[half, rows_of(j)] * (new_h - theta * new_x)
                x[half, rows_of(j)] = new_x
                h[half, rows_of(j)] = new_h
                t[half, rows_of(j)] = new_t
                tb[rows_of(j), half * HALF : (half + 1) * HALF] = new_t.astype(BF16)
        return new_ritz

    ritz = lax.fori_loop(0, ITERS, round_body, jnp.zeros((1, 1), F32))

    last = ITERS
    raise_inner()
    inn[0:512] = dot(tb[...], rt[:, 512:768]).astype(BF16)
    inn[512:1024] = dot(tb[...], rt[:, 768:1024]).astype(BF16)

    upper_arrive(last, False)
    praise[...] = dot(lr[...], in1[...])
    acc[...] = dot(lo[:, 0:1024], inn[0:1024])

    def last_own(j, part):
        return part + 2.0 * fold(acc[rows_of(j)] * t[c, rows_of(j)])

    part = lax.fori_loop(0, NX, last_own, jnp.zeros((1, 128), F32))
    upper_own(last)

    def last_part(j, total):
        return total + 2.0 * fold(praise[rows_of(j)] * tu[c, rows_of(j)])

    part = lax.fori_loop(0, NX, last_part, part)
    sums_out(last, local_sums(part))

    def drain_round(r, _):
        for j in range(NX):
            rcopy(sr.at[r, rows_of(j)], rr.at[r, rows_of(j)], sr_s.at[r, j], rr_r.at[r, j], (g, above)).wait_send()
            home = gown.at[r, c, rows_of(px)]
            rcopy(home, home, ownc_s.at[r, j], ownc_r.at[r, px], partner).wait_send()
        for k in range(1, NX):
            j = xoff(k)
            rcopy(so.at[r, rows_of(j)], ro.at[r, px], so_s.at[r, j], ro_r.at[r, px], xdev(j, s)).wait_send()
            rcopy(home, home, own_s.at[r, k], own_r.at[r, px], xdev(j, s)).wait_send()
        return 0

    def drain_upper(r, _):
        for j in range(NX):
            there = gup.at[r, c, rows_of(j)]
            rcopy(there, there, up_s.at[r, j], up_r.at[r, j], (g, below)).wait_send()

            @pl.when(r < ITERS)
            def _():
                rcopy(there, there, upc_s.at[r, j], upc_r.at[r, j], partner).wait_send()

        return 0

    def drain_sums(r, _):
        sums_drain(r)
        column_drain(r)
        return 0

    lax.fori_loop(0, ITERS, drain_round, 0)
    rows_out(last)
    lax.fori_loop(0, ITERS + 1, drain_upper, 0)
    for copy in env:
        copy.wait_send()
    k_copy.wait_send()
    k_forward.wait_send()

    column_out(last)
    lax.fori_loop(0, ITERS, drain_sums, 0)
    sums_drain(last)
    set_coef(total_out(last), last, ritz)
    energies[last - 1] = coef[2]
    a0, d0 = coef[0], coef[1]

    writes = []
    for j in range(NX):
        for half in range(2):
            staged[rows_of(j), half * HALF : (half + 1) * HALF] = (
                a0 * x[half, rows_of(j)] + d0 * t[half, rows_of(j)]
            )
        writes.append(pltpu.make_async_copy(staged.at[rows_of(j)], out.at[rows_of(j)], load_sem.at[j]))
        writes[-1].start()

    column_drain(last)
    for copy in writes:
        copy.wait()


def body(left_env, right_env, guess, precond, sector_rows):
    sectors = lax.axis_size("sec")
    ny = min(NY, sectors)
    nz = sectors // ny
    rounds = ITERS + 1
    vm, dma = pltpu.VMEM, pltpu.SemaphoreType.DMA
    halves = (2, B, HALF)
    scratch = [
        vm((B, 1024), BF16), vm((B, 3072), BF16), vm((B, 1536), BF16), vm((B, 512), BF16), vm((4, HALF, B), BF16),
        vm(halves, F32), vm(halves, BF16), vm(halves, BF16), vm(halves, BF16),
        vm(halves, F32), vm(halves, F32), vm(halves, F32), vm(halves, F32), vm(halves, F32), vm(halves, F32),
        vm((B, B), BF16), vm((B, B), BF16),
        vm((ITERS,) + halves, BF16), vm((rounds,) + halves, BF16),
        vm((ITERS, B, HALF), BF16), vm((ITERS, B, HALF), BF16),
        vm((ITERS, NX, Q, HALF), BF16), vm((ITERS, B, HALF), BF16),
        vm((B, HALF), F32), vm((B, HALF), F32), vm((1024, HALF), BF16), vm((3072, HALF), BF16), vm((Q, HALF), F32), vm((B, B), F32),
        vm((rounds, 2 * NX, 8, 128), F32), vm((rounds, ny, 8, 128), F32),
        vm((rounds, nz, 8, 128), F32), vm((rounds, 8, 128), F32),
        pltpu.SMEM((4,), F32),
        dma((10,)), dma((6,)), dma((6,)), dma((2,)), dma((2,)),
        dma((rounds, NX)), dma((rounds, NX)), dma((rounds, NX)), dma((rounds, NX)),
        dma((ITERS, NX)), dma((ITERS, NX)), dma((ITERS, NX)), dma((ITERS, NX)),
        dma((ITERS, NX)), dma((ITERS, NX)), dma((ITERS, NX)), dma((ITERS, NX)),
        dma((rounds, NX)), dma((rounds, 2 * NX)), dma((rounds, ny)), dma((rounds, ny)),
        dma((rounds, nz)), dma((rounds, nz)), dma((rounds,)), dma((rounds,)),
    ]
    any_space = pl.BlockSpec(memory_space=pl.ANY)
    vector, energies = pl.pallas_call(
        functools.partial(kernel, sectors, ny, nz),
        out_shape=(jax.ShapeDtypeStruct((B, B), F32), jax.ShapeDtypeStruct((ITERS,), F32)),
        in_specs=[any_space] * 4 + [pl.BlockSpec(memory_space=pltpu.SMEM)],
        out_specs=(pl.BlockSpec(memory_space=pl.ANY), pl.BlockSpec(memory_space=pltpu.SMEM)),
        scratch_shapes=scratch,
        compiler_params=pltpu.CompilerParams(
            collective_id=0, has_side_effects=True, vmem_limit_bytes=56 * 1024 * 1024
        ),
        name="davidson",
    )(left_env, right_env, guess, precond, sector_rows)
    return vector * math.sqrt(float(B * B * sectors)), energies


def solution(mesh):
    in_specs = (
        P("grp", None, "sec", None),
        P("grp", None, "sec", None),
        P("sec", None),
        P("sec", None),
        P("sec"),
    )
    out_specs = (P("sec", None), P())
    return jax.shard_map(body, mesh=mesh, in_specs=in_specs, out_specs=out_specs, check_vma=False)
```
